128 devices in a mesh: gz: 16 (over x, z_hi, core), gy: 8 (over z_lo, y).
Axes of the slice: x: 4, y: 4, z: 4 (z_hi: 2, z_lo: 2; z = z_hi * 2 + z_lo), core: 2. Of those that a mesh axis runs over, the one named last changes fastest.
Arguments:
- noisy: float32 [64, 512, 512], P('gz', 'gy'), may hold values from -6 to 6
- noise: float32 [64, 512, 512], P(None, 'gy', 'gz'), may hold values from -6 to 6
- timestep: int32 [1], replicated, may hold values from 100 to 599
- measured: float32 [4, 2, 512, 512], P(None, None, 'gz', 'gy'), may hold values from -6 to 6
- cap_index: int32 [4, 512, 512], P(None, 'gz', 'gy'), may hold values from 0 to 63, as said below
- w_patch: bfloat16 [2, 256, 384], replicated, may hold values from -0.375 to 0.375
- w_qkv: bfloat16 [2, 384, 1152], replicated, may hold values from -40 to 40
- w_out: bfloat16 [2, 384, 384], replicated, may hold values from -0.3125 to 0.3125
- w_up: bfloat16 [2, 384, 1536], replicated, may hold values from -0.3125 to 0.3125
- w_down: bfloat16 [2, 1536, 384], replicated, may hold values from -0.15625 to 0.15625
- w_unpatch: bfloat16 [2, 384, 256], replicated, may hold values from -0.3125 to 0.3125
- norm_gain: float32 [2, 3, 384], replicated, may hold values from 0.25 to 1.75
Outputs:
- previous: float32 [64, 512, 512], P(None, 'gy', 'gz')
- estimate: float32 [64, 512, 512], P(None, 'gy', 'gz')
The draws below stay inside these ranges and needn't reach their ends.
Inputs may be any that keep to these rules, and one draw needn't show every extreme that they name: cap_index[a, ky, kx] is the depth frequency that illumination a measures at lateral frequencies ky, kx; different illuminations may name the same cell.
All inputs are finite; a program needn't handle non-finite values.
Results may differ from the reference program's by a relative error of at most 0.011.
Values may be sent and summed in bfloat16 or wider, within the bound.
A program may use at most 128 MiB of HBM per device.

```python
import math
import jax
import jax.numpy as jnp
from jax import lax

LAT = 512
PATCH = 16
D = 384
HEADS = 6
FF = 1536
NA = 4
TRAIN_STEPS = 1000
STRIDE = 100
NZ = 64


def draw_cap_index(key, part):
    key = jax.random.fold_in(key, 9)
    subkeys = jax.random.split(key, 3)
    centre_y = jax.random.randint(subkeys[0], (NA, 1, 1), -(LAT // 8), LAT // 8 + 1)
    centre_x = jax.random.randint(subkeys[1], (NA, 1, 1), -(LAT // 8), LAT // 8 + 1)
    lowest = -jax.random.randint(subkeys[2], (NA, 1, 1), 1, NZ // 4 + 1)
    frequency = jnp.arange(LAT, dtype=jnp.int32)
    signed = jnp.where(frequency < LAT // 2, frequency, frequency - LAT)
    radius_sq = (signed[None, :, None] - centre_y) ** 2 + (signed[None, None, :] - centre_x) ** 2
    return ((lowest + radius_sq // (2 * NZ)) % NZ).astype(jnp.int32)


def draw_w_qkv(key, part):
    key = jax.random.fold_in(key, 5)
    base_draw = jax.random.normal(key, (2, D, 3 * D), jnp.float32) / math.sqrt(D)
    return base_draw.astype(jnp.bfloat16)


def block_levels(key, extent, pieces, smallest, top_value):
    def one(position, parts):
        draws = jax.random.uniform(jax.random.fold_in(jax.random.fold_in(key, 6), position), (parts,), jnp.float32, smallest / len(pieces), top_value / len(pieces))
        return jnp.repeat(jnp.exp(draws), extent[position] // parts).reshape((-1,) + (1,) * (len(extent) - position - 1))

    loudness = one(*pieces[0])
    for cut in pieces[1:]:
        loudness = loudness * one(*cut)
    return loudness


def gaussian(rng, shape, scale, bound, shards=(), kind=jnp.bfloat16):
    values = scale * jax.random.normal(rng, shape, jnp.float32)
    if shards:
        values = values * block_levels(rng, shape, shards, -0.22, 0.18)
    return jnp.clip(values, -bound, bound).astype(kind)


def setup_inputs(seed: int = 0) -> dict:
    splits = jax.random.split(jax.random.key(seed), 13)
    noisy = gaussian(splits[0], (NZ, LAT, LAT), 1.0, 6.0, ((0, 16), (1, 8)), jnp.float32)
    noise = gaussian(splits[1], (NZ, LAT, LAT), 1.0, 6.0, ((1, 8), (2, 16)), jnp.float32)
    timestep = jax.random.randint(splits[2], (1,), STRIDE, 600).astype(jnp.int32)
    measured = gaussian(splits[3], (NA, 2, LAT, LAT), 1.0, 6.0, ((2, 16), (3, 8)), jnp.float32)
    cap_index = draw_cap_index(jax.random.fold_in(splits[12], 71), 0)
    w_patch = gaussian(splits[5], (2, PATCH * PATCH, D), (PATCH * PATCH) ** -0.5, 0.375)
    w_qkv = draw_w_qkv(jax.random.fold_in(splits[12], 71), 0)
    w_out = gaussian(splits[7], (2, D, D), D ** -0.5, 0.3125)
    w_up = gaussian(splits[8], (2, D, FF), D ** -0.5, 0.3125)
    w_down = gaussian(splits[9], (2, FF, D), FF ** -0.5, 0.15625)
    w_unpatch = gaussian(splits[10], (2, D, PATCH * PATCH), D ** -0.5, 0.3125)
    norm_gain = jnp.clip(1.0 + 0.15 * jax.random.normal(splits[11], (2, 3, D), jnp.float32), 0.25, 1.75)
    return {"noisy": noisy, "noise": noise, "timestep": timestep, "measured": measured, "cap_index": cap_index, "w_patch": w_patch, "w_qkv": w_qkv, "w_out": w_out, "w_up": w_up, "w_down": w_down, "w_unpatch": w_unpatch, "norm_gain": norm_gain}


norm_eps = 1e-05

def widen(values):
    return lax.optimization_barrier(values).astype(jnp.float32)

def cumulative_alpha(moment):
    phase_angle = (moment / TRAIN_STEPS + 0.008) / 1.008 * (math.pi / 2.0)
    return jnp.cos(phase_angle) ** 2

def time_features(moment):
    half_width = D // 2
    frequency = jnp.exp(-math.log(10000.0) * jnp.arange(half_width).astype(jnp.float32) / half_width)
    angles = moment * frequency
    return jnp.concatenate([jnp.sin(angles), jnp.cos(angles)])

def layer_norm(values, gain_row):
    average = lax.optimization_barrier(jnp.mean(values, axis=-1, keepdims=True))
    centred = values - average
    variance = lax.optimization_barrier(jnp.mean(centred * centred, axis=-1, keepdims=True))
    return centred * lax.rsqrt(variance + norm_eps) * gain_row

def transformer(pixels, layers, gains, features):
    w_patch, w_qkv, w_out, w_up, w_down, w_unpatch = layers
    slices, tokens_per, pixel_count = pixels.shape
    head_size = D // HEADS
    flattened = pixels.reshape(slices * tokens_per, pixel_count).astype(jnp.bfloat16)
    hidden = jnp.dot(flattened, w_patch, preferred_element_type=jnp.float32) + features
    normed = layer_norm(hidden, gains[0]).astype(jnp.bfloat16)
    projected = jnp.dot(normed, w_qkv, preferred_element_type=jnp.float32).astype(jnp.bfloat16)
    projected = widen(projected).reshape(slices, tokens_per, 3, HEADS, head_size)
    queries = projected[:, :, 0]
    key_rows = projected[:, :, 1]
    value_rows = projected[:, :, 2]
    scores = jnp.einsum('sqhe,skhe->shqk', queries, key_rows) * (1.0 / math.sqrt(head_size))
    row_max = lax.optimization_barrier(jnp.max(scores, axis=-1, keepdims=True))
    raised = jnp.exp(scores - row_max)
    totals = lax.optimization_barrier(jnp.sum(raised, axis=-1))
    probs = widen(raised.astype(jnp.bfloat16))
    attended = jnp.einsum('shqk,skhe->sqhe', probs, value_rows)
    attended = attended / jnp.swapaxes(totals, 1, 2)[..., None]
    attended = attended.astype(jnp.bfloat16).reshape(slices * tokens_per, D)
    hidden = hidden + jnp.dot(attended, w_out, preferred_element_type=jnp.float32)
    normed = layer_norm(hidden, gains[1]).astype(jnp.bfloat16)
    inner_act = jax.nn.gelu(jnp.dot(normed, w_up, preferred_element_type=jnp.float32)).astype(jnp.bfloat16)
    hidden = hidden + jnp.dot(inner_act, w_down, preferred_element_type=jnp.float32)
    normed = layer_norm(hidden, gains[2]).astype(jnp.bfloat16)
    net_out = jnp.dot(normed, w_unpatch, preferred_element_type=jnp.float32)
    return net_out.reshape(slices, tokens_per, pixel_count)

def reference(noisy, noise, timestep, measured, cap_index, w_patch, w_qkv, w_out, w_up, w_down, w_unpatch, norm_gain):
    moment = timestep[0].astype(jnp.float32)
    signal_now = cumulative_alpha(moment)
    signal_prev = cumulative_alpha(moment - STRIDE)
    root_signal = jnp.sqrt(signal_now)
    root_noise = jnp.sqrt(1.0 - signal_now)
    features = time_features(moment)
    grid_side = LAT // PATCH

    def model_layers(model_index):
        return (w_patch[model_index], w_qkv[model_index], w_out[model_index], w_up[model_index], w_down[model_index], w_unpatch[model_index])
    depth_layers = model_layers(0)
    side_layers = model_layers(1)

    def depth_slice(image_slice):
        pixels = image_slice.reshape(1, grid_side, PATCH, grid_side, PATCH).transpose(0, 1, 3, 2, 4)
        pixels = pixels.reshape(1, grid_side * grid_side, PATCH * PATCH)
        net_out = transformer(pixels, depth_layers, norm_gain[0], features)
        return net_out.reshape(grid_side, grid_side, PATCH, PATCH).transpose(0, 2, 1, 3).reshape(LAT, LAT)
    depth_net = lax.map(depth_slice, noisy)
    first_guess = (noisy - root_noise * depth_net) / root_signal
    spectrum = jnp.fft.fftn(first_guess, norm='ortho')
    picked = jnp.take_along_axis(spectrum, cap_index, axis=0)
    residue = lax.complex(measured[:, 0], measured[:, 1]) - picked
    depth_ids = jnp.arange(NZ).astype(jnp.int32)[:, None, None]
    correction = jnp.zeros_like(spectrum)
    for illum in range(NA):
        correction = correction + jnp.where(depth_ids == cap_index[illum][None], residue[illum][None], 0.0)
    blended = first_guess + jnp.real(jnp.fft.ifftn(correction, norm='ortho'))

    def side_group(images):
        group_size = images.shape[0]
        pixels = images.reshape(group_size, grid_side, PATCH, NZ // PATCH, PATCH).transpose(0, 1, 3, 2, 4)
        pixels = pixels.reshape(group_size, grid_side * (NZ // PATCH), PATCH * PATCH)
        net_out = transformer(pixels, side_layers, norm_gain[1], features)
        net_out = net_out.reshape(group_size, grid_side, NZ // PATCH, PATCH, PATCH).transpose(0, 1, 3, 2, 4)
        return net_out.reshape(group_size, LAT, NZ)
    side_view = jnp.transpose(blended, (2, 1, 0)).reshape(LAT // 4, 4, LAT, NZ)
    side_net = lax.map(side_group, side_view).reshape(LAT, LAT, NZ)
    estimate = blended + root_noise * jnp.transpose(side_net, (2, 1, 0))
    predicted_noise = (noisy - root_signal * estimate) / root_noise
    toward = jnp.sqrt((1.0 - signal_prev) * signal_now * (1.0 / signal_prev - 1.0) / (1.0 - signal_now))
    spread = jnp.sqrt((1.0 - signal_prev) / (1.0 - signal_now) * (1.0 - signal_now / signal_prev))
    previous = jnp.sqrt(signal_prev) * estimate + toward * predicted_noise + spread * noise
    return (previous, estimate)
```

```python
import functools
import math

import jax
import jax.numpy as jnp
import numpy as np
from jax import lax
from jax.experimental import pallas as pl
from jax.experimental.pallas import tpu as pltpu
from jax.sharding import PartitionSpec as P

PATCH = 16
D = 384
HEADS = 6
FF = 1536
TRAIN_STEPS = 1000
STRIDE = 100
NZ = 64
LAT = 512
GZ = 16
GY = 8
NY = 4
GROUP = GZ * NY
SIDE = LAT // PATCH
HALF = SIDE * SIDE // 2
PIX = PATCH * PATCH
norm_eps = 1e-05
MIB = 1024 * 1024
f32 = jnp.float32
bf16 = jnp.bfloat16
MESH_ID = pl.DeviceIdType.MESH
NT = (((1,), (1,)), ((), ()))
TN = (((0,), (0,)), ((), ()))


def tables():
    parity, half_x, block_y = np.meshgrid(np.arange(2), np.arange(16), np.arange(32), indexing="ij")
    block_x = (2 * half_x + parity).reshape(-1)
    block_y = block_y.reshape(-1)
    by, bx = np.meshgrid(np.arange(32), np.arange(32), indexing="ij")
    by, bx = by.reshape(-1), bx.reshape(-1)
    turn = 2 * np.pi * ((block_y[:, None] * by[None] + block_x[:, None] * bx[None]) % 32) / 32
    coarse = np.concatenate([np.cos(turn), -np.sin(turn)], axis=1)
    xi, yi = np.meshgrid(np.arange(16), np.arange(16), indexing="ij")
    xi, yi = xi.reshape(-1), yi.reshape(-1)
    turn = 2 * np.pi * ((yi[:, None] * by[None] + xi[:, None] * bx[None]) % 512) / 512
    twist = np.stack([np.cos(turn), -np.sin(turn)]) / 32.0
    fine = np.zeros((2, 16, 4, 2, 2, 2, 256))
    for half in range(2):
        for quarter in range(4):
            for rest in range(2):
                ax = 8 * half + 2 * quarter + rest
                turn = 2 * np.pi * ((np.arange(16)[:, None] * yi[None] + ax * xi[None]) % 16) / 16
                fine[half, :, quarter, 0, rest, 0] = np.cos(turn)
                fine[half, :, quarter, 0, rest, 1] = np.sin(turn)
                fine[half, :, quarter, 1, rest, 0] = -np.sin(turn)
                fine[half, :, quarter, 1, rest, 1] = np.cos(turn)
    fine = fine.reshape(2, 256, 512) / 16.0
    to_bf = lambda a: a.astype(jnp.bfloat16)
    order = np.zeros((512, 512), np.float32)
    for gy in range(8):
        for hx in range(16):
            for yb in range(4):
                order[hx * 32 + gy * 4 + yb, gy * 64 + hx * 4 + yb] = 1.0
    swap = np.zeros((256, 256), np.float32)
    for y in range(16):
        for x in range(16):
            swap[x * 16 + y, y * 16 + x] = 1.0
    return (
        to_bf(coarse),
        twist.astype(np.float32),
        to_bf(fine),
        to_bf(np.ascontiguousarray(fine.transpose(0, 2, 1))),
        to_bf(order),
        to_bf(swap),
    )


def cumulative_alpha(moment):
    phase_angle = (moment / TRAIN_STEPS + 0.008) / 1.008 * (math.pi / 2.0)
    return jnp.cos(phase_angle) ** 2


def time_features(moment):
    half_width = D // 2
    frequency = jnp.exp(
        -math.log(10000.0) * jnp.arange(half_width).astype(jnp.float32) / half_width
    )
    angles = moment * frequency
    return jnp.concatenate([jnp.sin(angles), jnp.cos(angles)])


def dot(a, b, dims=None):
    if dims is None:
        return jnp.dot(a, b, preferred_element_type=f32)
    return lax.dot_general(a, b, dims, preferred_element_type=f32)


def norm(values, gain_row):
    average = jnp.mean(values, axis=-1, keepdims=True)
    centred = values - average
    variance = jnp.mean(centred * centred, axis=-1, keepdims=True)
    return (centred * lax.rsqrt(variance + norm_eps) * gain_row).astype(bf16)


def gelu(v):
    return 0.5 * v * (1.0 + jnp.tanh(math.sqrt(2.0 / math.pi) * (v + 0.044715 * (v * v * v))))


def group_kernel(src, dst, send_sem, recv_sem, local_sem):
    gz, gy = lax.axis_index("gz"), lax.axis_index("gy")
    plane, y = gy // NY, gy % NY
    me = gz * NY + y

    def place(k):
        peer = lax.rem(me + k, GROUP)
        return peer, {"gz": peer // NY, "gy": plane * NY + peer % NY}

    barrier = pltpu.get_barrier_semaphore()

    @pl.loop(1, GROUP)
    def _(k):
        _, where = place(k)
        pl.semaphore_signal(barrier, inc=1, device_id=where, device_id_type=MESH_ID)

    pl.semaphore_wait(barrier, GROUP - 1)
    own = pltpu.make_async_copy(src.at[me], dst.at[me], local_sem)
    own.start()

    @pl.loop(1, GROUP)
    def _(k):
        peer, where = place(k)
        pltpu.make_async_remote_copy(
            src_ref=src.at[peer],
            dst_ref=dst.at[me],
            send_sem=send_sem,
            recv_sem=recv_sem,
            device_id=where,
            device_id_type=MESH_ID,
        ).start()

    own.wait()
    part = pl.ds(0, GROUP - 1)
    pltpu.make_async_copy(src.at[part], src.at[part], send_sem).wait()
    pltpu.make_async_copy(dst.at[part], dst.at[part], recv_sem).wait()


def gy_kernel(src, dst, send_sem, recv_sem, local_sem):
    me = lax.axis_index("gy")
    barrier = pltpu.get_barrier_semaphore()
    for k in range(1, GY):
        pl.semaphore_signal(
            barrier, inc=1, device_id={"gy": lax.rem(me + k, GY)}, device_id_type=MESH_ID
        )
    pl.semaphore_wait(barrier, GY - 1)
    own = pltpu.make_async_copy(src.at[me], dst.at[me], local_sem)
    own.start()
    for k in range(1, GY):
        peer = lax.rem(me + k, GY)
        pltpu.make_async_remote_copy(
            src_ref=src.at[peer],
            dst_ref=dst.at[me],
            send_sem=send_sem,
            recv_sem=recv_sem,
            device_id={"gy": peer},
            device_id_type=MESH_ID,
        ).start()
    own.wait()
    part = pl.ds(0, GY - 1)
    pltpu.make_async_copy(src.at[part], src.at[part], send_sem).wait()
    pltpu.make_async_copy(dst.at[part], dst.at[part], recv_sem).wait()


def all_to_all(kernel, data, cid):
    return pl.pallas_call(
        kernel,
        out_shape=jax.ShapeDtypeStruct(data.shape, data.dtype),
        in_specs=[pl.BlockSpec(memory_space=pl.ANY)],
        out_specs=pl.BlockSpec(memory_space=pl.ANY),
        scratch_shapes=[pltpu.SemaphoreType.DMA] * 3,
        compiler_params=pltpu.CompilerParams(collective_id=cid, has_side_effects=True),
    )(data)


def pair_kernel(pick, src, dst, send_sem, recv_sem):
    gy = lax.axis_index("gy")
    plane = gy // NY
    other = {"gy": (1 - plane) * NY + gy % NY}
    barrier = pltpu.get_barrier_semaphore()
    pl.semaphore_signal(barrier, inc=1, device_id=other, device_id_type=MESH_ID)
    pl.semaphore_wait(barrier, 1)
    copy = pltpu.make_async_remote_copy(
        src_ref=src.at[1 - plane] if pick else src,
        dst_ref=dst,
        send_sem=send_sem,
        recv_sem=recv_sem,
        device_id=other,
        device_id_type=MESH_ID,
    )
    copy.start()
    copy.wait()


def pair_swap(data, pick, cid):
    return pl.pallas_call(
        functools.partial(pair_kernel, pick),
        out_shape=jax.ShapeDtypeStruct(data.shape[-2:], data.dtype),
        in_specs=[pl.BlockSpec(memory_space=pl.ANY)],
        out_specs=pl.BlockSpec(memory_space=pl.ANY),
        scratch_shapes=[pltpu.SemaphoreType.DMA] * 2,
        compiler_params=pltpu.CompilerParams(collective_id=cid, has_side_effects=True),
    )(data)


def call(kernel, outs, args, scratch=(), smem=(), limit=40):
    return pl.pallas_call(
        kernel,
        out_shape=outs,
        in_specs=[
            pl.BlockSpec(memory_space=pltpu.SMEM if i in smem else pltpu.VMEM)
            for i in range(len(args))
        ],
        out_specs=jax.tree.map(lambda _: pl.BlockSpec(memory_space=pltpu.VMEM), outs),
        scratch_shapes=list(scratch),
        compiler_params=pltpu.CompilerParams(vmem_limit_bytes=limit * MIB),
    )(*args)


def attention(queries, keys, values, rows, cols, left):
    outs = []
    for pair in range(HEADS // 2):
        lanes = slice(128 * pair, 128 * pair + 128)
        q, k, v = queries[:, lanes], keys[:, lanes], values[:, lanes]
        halves = []
        for which in range(2):
            q_one = jnp.where(left if which == 0 else ~left, q, jnp.zeros_like(q))
            scores = dot(q_one, k, NT)
            top = jnp.max(scores, axis=-1, keepdims=True)
            raised = jnp.exp(scores - top)
            total = jnp.sum(raised, axis=-1, keepdims=True)
            halves.append(dot(raised.astype(bf16), v) / total)
        outs.append(jnp.where(left, halves[0], halves[1]).astype(bf16))
    return jnp.concatenate(outs, axis=1)


def tail(hidden, attended, w_out, w_up, w_down, gains):
    hidden = hidden + dot(attended, w_out[...])
    normed = norm(hidden, gains[1:2, :])
    inner = gelu(dot(normed, w_up[...])).astype(bf16)
    hidden = hidden + dot(inner, w_down[...])
    return norm(hidden, gains[2:3, :])


def depth_kernel(
    scal, got, order, swap, feat, gains, w_patch, w_qkv, w_out, w_up, w_down, w_unpatch,
    guess, guess16, tok, low, hidden, queries, pairs,
):
    chunk = 256
    arrived = got[...].reshape(GY * 64, 768)
    tok[...] = dot(order[...], arrived[:, :256]).astype(bf16)
    low[...] = dot(order[...], arrived[:, 256:512]).astype(bf16)

    def own(i, _):
        at = pl.ds(pl.multiple_of(i * chunk, chunk), chunk)
        first = dot(tok[at, :], w_patch[...]) + feat[...]
        hidden[at, :] = first
        normed = norm(first, gains[0:1, :])
        queries[at, :] = (dot(normed, w_qkv[:, :D]).astype(bf16) * 0.125).astype(bf16)
        pairs[at, :] = dot(normed, w_qkv[:, D:]).astype(bf16)
        return 0

    lax.fori_loop(0, HALF // chunk, own, 0)

    def other(i, _):
        part = got[pl.ds(i * (chunk // 64), chunk // 64), :, 512:].reshape(chunk, 256)
        first = dot(part, w_patch[...]) + feat[...]
        normed = norm(first, gains[0:1, :])
        at = pl.ds(pl.multiple_of(HALF + i * chunk, chunk), chunk)
        pairs[at, :] = dot(normed, w_qkv[:, D:]).astype(bf16)
        return 0

    lax.fori_loop(0, HALF // chunk, other, 0)
    small = 128

    for i in range(HALF // small):
        at = slice(i * small, i * small + small)
        left = lax.broadcasted_iota(jnp.int32, (small, 128), 1) < 64
        attended = attention(
            queries[at, :], pairs[:, :D], pairs[:, D:], small, 2 * HALF, left
        )
        normed = tail(hidden[at, :], attended, w_out, w_up, w_down, gains)
        net = dot(w_unpatch[...], normed, (((0,), (1,)), ((), ())))
        value = dot(swap[...], tok[at, :], NT) + dot(swap[...], low[at, :], NT)
        first = (value - scal[0] * net) * scal[1]
        guess[:, at] = first
        guess16[:, at] = first.astype(bf16)


def forward_kernel(half, own, other, coarse, twist, fine, out, spread):
    one = jnp.where(half[0] == 0, own[...], other[...])
    two = jnp.where(half[0] == 0, other[...], own[...])
    both = jnp.concatenate([one, two], axis=1)
    width = 256
    for c in range(1024 // width):
        at = slice(c * width, c * width + width)
        real = dot(both, coarse[:, at])
        imag = dot(both, coarse[:, 1024 + c * width : 1024 + c * width + width])
        t_re, t_im = twist[0, :, at], twist[1, :, at]
        turned = jnp.concatenate(
            [(real * t_re - imag * t_im).astype(bf16), (real * t_im + imag * t_re).astype(bf16)],
            axis=0,
        )
        res = dot(fine[half[0]], turned)
        for k in range(width // 128):
            spread[pl.ds(c * (width // 128) + k, 256, stride=8), :] = res[:, 128 * k : 128 * k + 128]
    out[...] = spread[...].astype(bf16).reshape(GROUP, 2, 16, 128)


def cap_kernel(got, measured, cap, out):
    angle = cap[...].astype(f32) * (2.0 * math.pi / NZ)
    w_re, w_im = jnp.cos(angle), -jnp.sin(angle)

    def gather(i, state):
        p_re, p_im = state
        z = NZ - 1 - i
        x_re, x_im = got[z, 0].astype(f32), got[z, 1].astype(f32)
        return (
            p_re * w_re - p_im * w_im + x_re[None],
            p_re * w_im + p_im * w_re + x_im[None],
        )

    zero = jnp.zeros_like(w_re)
    p_re, p_im = lax.fori_loop(0, NZ, gather, (zero, zero), unroll=8)
    scale = 1.0 / math.sqrt(NZ)
    r_re = (measured[:, 0] - p_re * scale) * scale
    r_im = (measured[:, 1] - p_im * scale) * scale

    def expand(z, state):
        t_re, t_im = state
        out[z, 0] = (t_re[0] + t_re[1] + t_re[2] + t_re[3]).astype(bf16)
        out[z, 1] = (t_im[0] + t_im[1] + t_im[2] + t_im[3]).astype(bf16)
        return (t_re * w_re + t_im * w_im, t_im * w_re - t_re * w_im)

    lax.fori_loop(0, NZ, expand, (r_re, r_im), unroll=8)


def inverse_kernel(half, got, coarse, twist, fine_t, out, spread, turned):
    spread[...] = got[...].reshape(GROUP * 32, 128).astype(f32)
    for c in range(4):
        lanes = slice(c * 256, c * 256 + 256)
        cells = jnp.concatenate(
            [spread[pl.ds(2 * c + k, 256, stride=8), :].astype(bf16) for k in range(2)], axis=1
        )
        res = dot(fine_t[half[0]], cells)
        real, imag = res[:256], res[256:]
        t_re, t_im = twist[0, :, lanes], twist[1, :, lanes]
        turned[:, lanes] = (real * t_re + imag * t_im).astype(bf16)
        turned[:, 1024 + c * 256 : 1024 + c * 256 + 256] = (imag * t_re - real * t_im).astype(bf16)
    for c in range(4):
        back = dot(turned[...], coarse[c * 256 : c * 256 + 256, :], NT)
        out[c // 2, :, (c % 2) * 256 : (c % 2) * 256 + 256] = back.astype(bf16)


def blend_kernel(half, guess, own, other, out):
    mine = own[half[0]].astype(f32)
    blended = guess[...] + (mine + other[...].astype(f32))
    for q in range(4):
        rows = [blended[q * 64 + r * 16 : q * 64 + r * 16 + 16, :] for r in range(4)]
        for x in range(16):
            out[x * 4 + q] = jnp.concatenate(
                [row[:, 32 * x : 32 * x + 32] for row in rows], axis=1
            )


def side_kernel(
    scal, got, feat, gains, w_patch, w_qkv, w_out, w_up, w_down, w_unpatch,
    out, hidden, last,
):
    for zb in range(4):
        pix = got[zb * 16 : zb * 16 + 16].reshape(256, 128).astype(bf16)
        first = dot(pix, w_patch[...], TN) + feat[...]
        for x in range(4):
            hidden[x * 128 + zb * 32 : x * 128 + zb * 32 + 32, :] = first[32 * x : 32 * x + 32, :]
    left = lax.broadcasted_iota(jnp.int32, (128, 128), 1) < 64
    for x in range(4):
        at = slice(128 * x, 128 * x + 128)
        normed = norm(hidden[at, :], gains[0:1, :])
        projected = dot(normed, w_qkv[...]).astype(bf16)
        queries = (projected[:, :D] * 0.125).astype(bf16)
        attended = attention(
            queries, projected[:, D : 2 * D], projected[:, 2 * D :], 128, 128, left
        )
        normed = tail(hidden[at, :], attended, w_out, w_up, w_down, gains)
        for zb in range(4):
            last[zb * 128 + 32 * x : zb * 128 + 32 * x + 32, :] = normed[32 * zb : 32 * zb + 32, :]
    for zb in range(4):
        net = dot(w_unpatch[...], last[zb * 128 : zb * 128 + 128, :], (((0,), (1,)), ((), ())))
        pix = got[zb * 16 : zb * 16 + 16].reshape(256, 128)
        out[zb * 16 : zb * 16 + 16] = (pix + scal[0] * net).reshape(16, 16, 128)


def local(
    noisy, noise, timestep, measured, cap_index, w_patch, w_qkv, w_out, w_up, w_down, w_unpatch,
    norm_gain,
):
    coarse, twist, fine, fine_t, order, swap = (jnp.asarray(t) for t in tables())
    moment = timestep[0].astype(f32)
    signal_now = cumulative_alpha(moment)
    signal_prev = cumulative_alpha(moment - STRIDE)
    root_signal = jnp.sqrt(signal_now)
    root_noise = jnp.sqrt(1.0 - signal_now)
    features = time_features(moment)[None]
    scal = jnp.stack([root_noise, 1.0 / root_signal])
    half = (lax.axis_index("gy") // NY).astype(jnp.int32)[None]

    cut = noisy.reshape(4, 4, 16, 16, 2, 16).transpose(4, 0, 3, 1, 2, 5).reshape(2, 4, 64, 256)
    high = cut.astype(bf16)
    low = (cut - high.astype(f32)).astype(bf16)
    send = jnp.concatenate([high, low, high[::-1]], axis=-1).reshape(GY, 64, 768)
    got = all_to_all(gy_kernel, send, 0)
    relayed = lax.all_to_all(noisy, "gz", split_axis=2, concat_axis=0, tiled=True)

    guess, guess16 = call(
        depth_kernel,
        (
            jax.ShapeDtypeStruct((PIX, HALF), f32),
            jax.ShapeDtypeStruct((PIX, HALF), bf16),
        ),
        (
            scal, got, order, swap, features, norm_gain[0], w_patch[0], w_qkv[0], w_out[0],
            w_up[0], w_down[0],
            w_unpatch[0].reshape(D, 16, 16).transpose(0, 2, 1).reshape(D, PIX),
        ),
        scratch=(
            pltpu.VMEM((HALF, PIX), bf16),
            pltpu.VMEM((HALF, PIX), bf16),
            pltpu.VMEM((HALF, D), f32),
            pltpu.VMEM((HALF, D), bf16),
            pltpu.VMEM((2 * HALF, 2 * D), bf16),
        ),
        smem=(0,),
    )
    other = pair_swap(guess16, False, 1)
    spectrum = call(
        forward_kernel,
        jax.ShapeDtypeStruct((GROUP, 2, 16, 128), bf16),
        (half, guess16, other, coarse, twist, fine),
        scratch=(pltpu.VMEM((GROUP * 32, 128), f32),),
        smem=(0,),
    )
    lines = all_to_all(group_kernel, spectrum, 2)
    cells = lambda a: a.reshape(a.shape[:-2] + (8, 4, 2, 32))
    meas = cells(measured).transpose(0, 1, 4, 2, 3, 5).reshape(4, 2, 16, 128)
    caps = cells(cap_index).transpose(0, 3, 1, 2, 4).reshape(4, 16, 128)
    fixed = call(
        cap_kernel, jax.ShapeDtypeStruct((GROUP, 2, 16, 128), bf16), (lines, meas, caps)
    )
    fixed = all_to_all(group_kernel, fixed, 3)
    back = call(
        inverse_kernel,
        jax.ShapeDtypeStruct((2, PIX, HALF), bf16),
        (half, fixed, coarse, twist, fine_t),
        scratch=(pltpu.VMEM((GROUP * 32, 128), f32), pltpu.VMEM((PIX, 2048), bf16)),
        smem=(0,),
    )
    other = pair_swap(back, True, 4)
    blended = call(
        blend_kernel,
        jax.ShapeDtypeStruct((GROUP, 16, 128), f32),
        (half, guess, back, other),
        smem=(0,),
    )
    columns = all_to_all(group_kernel, blended, 5)
    estimate = call(
        side_kernel,
        jax.ShapeDtypeStruct((NZ, 16, 128), f32),
        (
            scal, columns, features, norm_gain[1],
            w_patch[1].reshape(16, 16, D).transpose(1, 0, 2).reshape(PIX, D),
            w_qkv[1], w_out[1], w_up[1], w_down[1],
            w_unpatch[1].reshape(D, 16, 16).transpose(0, 2, 1).reshape(D, PIX),
        ),
        scratch=(pltpu.VMEM((512, D), f32), pltpu.VMEM((512, D), bf16)),
        smem=(0,),
    )
    parts = estimate.reshape(NZ, 16, 4, GY, 4).transpose(3, 0, 4, 1, 2).reshape(GY, NZ * 4 * 16, 4)
    parts = lax.all_to_all(parts, "gy", split_axis=0, concat_axis=0, tiled=True)
    estimate = parts.reshape(GY, NZ, 64, 4).transpose(1, 2, 0, 3).reshape(NZ, 64, 32)
    predicted_noise = (relayed - root_signal * estimate) / root_noise
    toward = jnp.sqrt(
        (1.0 - signal_prev) * signal_now * (1.0 / signal_prev - 1.0) / (1.0 - signal_now)
    )
    spread = jnp.sqrt((1.0 - signal_prev) / (1.0 - signal_now) * (1.0 - signal_now / signal_prev))
    previous = jnp.sqrt(signal_prev) * estimate + toward * predicted_noise + spread * noise
    return (previous, estimate)


def solution(mesh):
    placed = (
        P("gz", "gy", None),
        P(None, "gy", "gz"),
        P(),
        P(None, None, "gz", "gy"),
        P(None, "gz", "gy"),
    ) + (P(),) * 7
    return jax.shard_map(
        local,
        mesh=mesh,
        in_specs=placed,
        out_specs=(P(None, "gy", "gz"), P(None, "gy", "gz")),
        check_vma=False,
    )
```

```python
import math

import jax
import jax.numpy as jnp
import numpy as np
from jax import lax
from jax.experimental import pallas as pl
from jax.experimental.pallas import tpu as pltpu
from jax.sharding import PartitionSpec as P

PATCH = 16
D = 384
HEADS = 6
FF = 1536
TRAIN_STEPS = 1000
STRIDE = 100
NZ = 64
LAT = 512
GZ = 16
GY = 8
NY = 4
GROUP = GZ * NY
SIDE = LAT // PATCH
HALF = SIDE * SIDE // 2
PIX = PATCH * PATCH
norm_eps = 1e-05
MIB = 1024 * 1024
f32 = jnp.float32
bf16 = jnp.bfloat16
MESH_ID = pl.DeviceIdType.MESH
NT = (((1,), (1,)), ((), ()))
TN = (((0,), (0,)), ((), ()))


def tables():
    parity, half_x, block_y = np.meshgrid(np.arange(2), np.arange(16), np.arange(32), indexing="ij")
    block_x = (2 * half_x + parity).reshape(-1)
    block_y = block_y.reshape(-1)
    by, bx = np.meshgrid(np.arange(32), np.arange(32), indexing="ij")
    by, bx = by.reshape(-1), bx.reshape(-1)
    turn = 2 * np.pi * ((block_y[:, None] * by[None] + block_x[:, None] * bx[None]) % 32) / 32
    coarse = np.concatenate([np.cos(turn), -np.sin(turn)], axis=1)
    xi, yi = np.meshgrid(np.arange(16), np.arange(16), indexing="ij")
    xi, yi = xi.reshape(-1), yi.reshape(-1)
    turn = 2 * np.pi * ((yi[:, None] * by[None] + xi[:, None] * bx[None]) % 512) / 512
    twist = np.stack([np.cos(turn), -np.sin(turn)]) / 32.0
    fine = np.zeros((2, 16, 4, 2, 2, 2, 256))
    for half in range(2):
        for quarter in range(4):
            for rest in range(2):
                ax = 8 * half + 2 * quarter + rest
                turn = 2 * np.pi * ((np.arange(16)[:, None] * yi[None] + ax * xi[None]) % 16) / 16
                fine[half, :, quarter, 0, rest, 0] = np.cos(turn)
                fine[half, :, quarter, 0, rest, 1] = np.sin(turn)
                fine[half, :, quarter, 1, rest, 0] = -np.sin(turn)
                fine[half, :, quarter, 1, rest, 1] = np.cos(turn)
    fine = fine.reshape(2, 256, 512) / 16.0
    to_bf = lambda a: a.astype(jnp.bfloat16)
    order = np.zeros((512, 512), np.float32)
    for gy in range(8):
        for hx in range(16):
            for yb in range(4):
                order[hx * 32 + gy * 4 + yb, gy * 64 + hx * 4 + yb] = 1.0
    swap = np.zeros((256, 256), np.float32)
    for y in range(16):
        for x in range(16):
            swap[x * 16 + y, y * 16 + x] = 1.0
    cast = np.zeros((512, 512), np.float32)
    for xb in range(32):
        for s in range(4):
            for yb in range(4):
                cast[(xb % 2) * 256 + s * 64 + (xb // 2) * 4 + yb, xb * 16 + s * 4 + yb] = 1.0
    deal = np.zeros((512, 512), np.float32)
    for zb in range(4):
        for x in range(4):
            for yb in range(32):
                row = (yb // 4) * 64 + zb * 16 + (yb % 4) * 4 + x
                deal[row, zb * 128 + x * 32 + yb] = 1.0
    return (
        to_bf(coarse),
        twist.astype(np.float32),
        to_bf(fine),
        to_bf(np.ascontiguousarray(fine.transpose(0, 2, 1))),
        to_bf(order),
        to_bf(swap),
        to_bf(cast),
        to_bf(deal),
    )


def cumulative_alpha(moment):
    phase_angle = (moment / TRAIN_STEPS + 0.008) / 1.008 * (math.pi / 2.0)
    return jnp.cos(phase_angle) ** 2


def time_features(moment):
    half_width = D // 2
    frequency = jnp.exp(
        -math.log(10000.0) * jnp.arange(half_width).astype(jnp.float32) / half_width
    )
    angles = moment * frequency
    return jnp.concatenate([jnp.sin(angles), jnp.cos(angles)])


def dot(a, b, dims=None):
    if dims is None:
        return jnp.dot(a, b, preferred_element_type=f32)
    return lax.dot_general(a, b, dims, preferred_element_type=f32)


def norm(values, gain_row):
    average = jnp.mean(values, axis=-1, keepdims=True)
    centred = values - average
    variance = jnp.mean(centred * centred, axis=-1, keepdims=True)
    return (centred * lax.rsqrt(variance + norm_eps) * gain_row).astype(bf16)


def gelu(v):
    return 0.5 * v * (1.0 + jnp.tanh(math.sqrt(2.0 / math.pi) * (v + 0.044715 * (v * v * v))))


def exchange_blocks(arrays, width):
    arrays = list(arrays)
    lane = lax.broadcasted_iota(jnp.int32, arrays[0].shape, 1) // width
    step = 1
    while step < len(arrays):
        low = (lane // step) % 2 == 0
        for i in range(len(arrays)):
            if i & step == 0:
                a, b = arrays[i], arrays[i | step]
                arrays[i] = jnp.where(low, a, pltpu.roll(b, step * width, axis=1))
                arrays[i | step] = jnp.where(low, pltpu.roll(a, 128 - step * width, axis=1), b)
        step *= 2
    return arrays


def attention(queries, keys, values, left):
    outs = []
    for pair in range(HEADS // 2):
        lanes = slice(128 * pair, 128 * pair + 128)
        q, k, v = queries[:, lanes], keys[:, lanes], values[:, lanes]
        halves = []
        for which in range(2):
            q_one = jnp.where(left if which == 0 else ~left, q, jnp.zeros_like(q))
            scores = dot(q_one, k, NT)
            top = jnp.max(scores, axis=-1, keepdims=True)
            raised = jnp.exp(scores - top)
            total = jnp.sum(raised, axis=-1, keepdims=True)
            halves.append(dot(raised.astype(bf16), v) / total)
        outs.append(jnp.where(left, halves[0], halves[1]).astype(bf16))
    return jnp.concatenate(outs, axis=1)


def tail(hidden, attended, w_out, w_up, w_down, gains):
    hidden = hidden + dot(attended, w_out[...])
    normed = norm(hidden, gains[1:2, :])
    inner = gelu(dot(normed, w_up[...])).astype(bf16)
    hidden = hidden + dot(inner, w_down[...])
    return norm(hidden, gains[2:3, :])


CHUNK = 128
PARTS = HALF // CHUNK


def step_kernel(*refs):
    (
        scal, feat, gains, noisy, measured, cap,
        h_patch, h_qkv, h_out, h_up, h_down, h_unpatch,
        h_coarse, h_twist, h_fine, h_fine_t, h_order, h_swap, h_cast, h_deal,
        final_dst, relay_dst,
        patch0, qkv0, out0, up0, down0, unpatch0,
        patch1, qkv1, out1, up1, down1, unpatch1,
        coarse, twist, fine, fine_t, order, swap, cast, deal,
        strips, wide, cut, own_src, own_dst, oth_dst, relay_src,
        tok, low, hidden, queries, pairs, guess, guess16, guess_dst,
        summed, turned, spread, line_src, line_dst,
        cells, fix_src, fix_dst, turned2, spread2, back_src, back_dst, blended,
        col_src, col_dst, rest_src, rest_dst, last, final_src,
        load_sem, send_sem, recv_sem, pair_send, pair_recv,
    ) = refs
    gz, gy = lax.axis_index("gz"), lax.axis_index("gy")
    plane, y = gy // NY, gy % NY
    me = gz * NY + y

    plan = [
        (h_cast, cast), (h_swap, swap), (h_order, order), (h_patch.at[0], patch0),
        (h_qkv.at[0], qkv0), (h_out.at[0], out0), (h_up.at[0], up0), (h_down.at[0], down0),
        (h_unpatch.at[0], unpatch0), (h_coarse, coarse), (h_twist, twist),
        (h_fine.at[plane], fine), (h_fine_t.at[plane], fine_t),
        (h_patch.at[1], patch1), (h_qkv.at[1], qkv1), (h_out.at[1], out1), (h_up.at[1], up1),
        (h_down.at[1], down1), (h_unpatch.at[1], unpatch1), (h_deal, deal),
    ]
    loads = [
        pltpu.make_async_copy(src, dst, load_sem.at[i]) for i, (src, dst) in enumerate(plan)
    ]
    for load in loads:
        load.start()

    def in_group(k):
        peer = lax.rem(me + k, GROUP)
        return peer, {"gz": peer // NY, "gy": plane * NY + lax.rem(peer, NY)}

    def in_other_plane(k):
        return {"gy": (1 - plane) * NY + lax.rem(y + k, NY)}

    barrier = pltpu.get_barrier_semaphore()
    for k in range(NY):
        pl.semaphore_signal(
            barrier, inc=1, device_id=in_other_plane(k), device_id_type=MESH_ID
        )

    @pl.loop(1, GROUP)
    def _(k):
        _, where = in_group(k)
        pl.semaphore_signal(barrier, inc=1, device_id=where, device_id_type=MESH_ID)

    def remote(src, dst, send, recv, where):
        return pltpu.make_async_remote_copy(
            src_ref=src, dst_ref=dst, send_sem=send, recv_sem=recv,
            device_id=where, device_id_type=MESH_ID,
        )

    for g in range(4):
        strips[g] = noisy[:, 128 * g : 128 * g + 128]
        for part in range(2):
            rows = [strips[g, pl.ds(8 * part + i, 16, stride=16), :] for i in range(8)]
            for i, block in enumerate(exchange_blocks(rows, 16)):
                high = block.astype(bf16)
                at = slice((8 * g + i) * 16, (8 * g + i) * 16 + 16)
                cut[at, 128 * part : 128 * part + 128] = high
                cut[at, 256 + 128 * part : 384 + 128 * part] = (
                    block - high.astype(f32)
                ).astype(bf16)
    loads[0].wait()
    own_src[...] = dot(cast[...], cut[...]).astype(bf16).reshape(GY, 64, 512)

    pl.semaphore_wait(barrier, GROUP - 1 + NY)
    peers = []
    for k in range(1, GY):
        peer = lax.rem(gy + k, GY)
        where = {"gy": peer}
        flip = lax.rem(peer + NY, GY)
        peers.append((peer, where))
        remote(own_src.at[peer], own_dst.at[gy], send_sem.at[0], recv_sem.at[0], where).start()
        remote(
            own_src.at[flip, :, pl.ds(0, 256)], oth_dst.at[gy], send_sem.at[1], recv_sem.at[1],
            where,
        ).start()
    own_dst[gy] = own_src[gy]
    oth_dst[gy] = own_src[lax.rem(gy + NY, GY), :, 0:256]

    for s in range(2):
        for g in range(4):
            part = noisy[128 * s : 128 * s + 128, 128 * g : 128 * g + 128].T
            relay_src[4 * g : 4 * g + 4, :, 128 * s : 128 * s + 128] = part.reshape(4, 32, 128)

    @pl.loop(1, GZ)
    def _(k):
        peer = lax.rem(gz + k, GZ)
        remote(
            relay_src.at[peer], relay_dst.at[gz], send_sem.at[2], recv_sem.at[2], {"gz": peer}
        ).start()

    relay_dst[gz] = relay_src[gz]

    for a in range(12):
        wide[a, :, 0:64] = measured[a] if a < 8 else cap[a - 8].astype(f32)
        quarter = [wide[a, pl.ds(q, 8, stride=4), :] for q in range(4)]
        for r in range(2):
            cells[a, 8 * r : 8 * r + 8, :] = jnp.concatenate(
                [v[:, 32 * r : 32 * r + 32] for v in quarter], axis=1
            )

    for load in loads[1:9]:
        load.wait()
    unpatch0[...] = dot(unpatch0[...], swap[...]).astype(bf16)

    def gather(dst, src, s, r, count):
        part = pl.ds(0, count)
        del src
        pltpu.make_async_copy(dst.at[part], dst.at[part], recv_sem.at[r]).wait()

    gather(own_dst, None, 0, 0, GY - 1)
    gather(oth_dst, None, 1, 1, GY - 1)
    arrived = own_dst[...].reshape(GY * 64, 512)
    tok[...] = dot(order[...], arrived[:, :256]).astype(bf16)
    low[...] = dot(order[...], arrived[:, 256:]).astype(bf16)
    gain0 = gains.at[0]

    @pl.loop(0, 2)
    def _(i):
        at = pl.ds(pl.multiple_of(i * 256, 256), 256)
        first = dot(tok[at, :], patch0[...]) + feat[...]
        hidden[at, :] = first
        normed = norm(first, gain0[0:1, :])
        queries[at, :] = (dot(normed, qkv0[:, :D]).astype(bf16) * 0.125).astype(bf16)
        pairs[at, :] = dot(normed, qkv0[:, D:]).astype(bf16)

    @pl.loop(0, 2)
    def _(i):
        part = oth_dst[pl.ds(i * 4, 4)].reshape(256, 256)
        normed = norm(dot(part, patch0[...]) + feat[...], gain0[0:1, :])
        at = pl.ds(pl.multiple_of(HALF + i * 256, 256), 256)
        pairs[at, :] = dot(normed, qkv0[:, D:]).astype(bf16)

    partner = in_other_plane(0)
    left = lax.broadcasted_iota(jnp.int32, (CHUNK, 128), 1) < 64

    @pl.loop(0, PARTS)
    def _(i):
        at = pl.ds(pl.multiple_of(i * CHUNK, CHUNK), CHUNK)
        attended = attention(queries[at, :], pairs[:, :D], pairs[:, D:], left)
        normed = tail(hidden[at, :], attended, out0, up0, down0, gain0)
        net = dot(unpatch0[...], normed, (((0,), (1,)), ((), ())))
        value = dot(swap[...], tok[at, :], NT) + dot(swap[...], low[at, :], NT)
        first = (value - scal[0] * net) * scal[1]
        guess[:, at] = first
        guess16[i] = first.astype(bf16)
        remote(
            guess16.at[i], guess_dst.at[i], pair_send.at[i], pair_recv.at[i], partner
        ).start()

    for load in loads[9:13]:
        load.wait()
    half_rows = pl.ds(pl.multiple_of(plane * HALF, HALF), HALF)
    side_rows = pl.ds(pl.multiple_of((1 - plane) * HALF, HALF), HALF)
    mine = jnp.concatenate([guess16[i] for i in range(PARTS)], axis=1)
    for c in range(4):
        at = slice(512 * c, 512 * c + 512)
        summed[:, at] = dot(mine, coarse[half_rows, at])
    for i in range(PARTS):
        remote(
            guess16.at[i], guess_dst.at[i], pair_send.at[i], pair_recv.at[i], partner
        ).wait()
    theirs = jnp.concatenate([guess_dst[i] for i in range(PARTS)], axis=1)
    for c in range(4):
        at = slice(256 * c, 256 * c + 256)
        im = slice(1024 + 256 * c, 1280 + 256 * c)
        real = summed[:, at] + dot(theirs, coarse[side_rows, at])
        imag = summed[:, im] + dot(theirs, coarse[side_rows, im])
        t_re, t_im = twist[0, :, at], twist[1, :, at]
        turned[0:256, at] = (real * t_re - imag * t_im).astype(bf16)
        turned[256:512, at] = (real * t_im + imag * t_re).astype(bf16)

    @pl.loop(0, 4)
    def _(i):
        block = lax.rem(i + gz // 4, 4)
        res = dot(fine[pl.ds(pl.multiple_of(block * 64, 64), 64), :], turned[...])
        for c in range(8):
            spread[pl.ds(c, 64, stride=8), :] = res[:, 128 * c : 128 * c + 128]
        line_src[pl.ds(block * 16, 16)] = spread[...].astype(bf16).reshape(16, 2, 16, 128)

        @pl.loop(0, 16)
        def _(j):
            peer = block * 16 + j

            @pl.when(peer != me)
            def _():
                where = {"gz": peer // NY, "gy": plane * NY + lax.rem(peer, NY)}
                remote(
                    line_src.at[peer], line_dst.at[me], send_sem.at[3], recv_sem.at[3], where
                ).start()

    line_dst[me] = line_src[me]

    angle = cells[8:12] * (2.0 * math.pi / NZ)
    w_re, w_im = jnp.cos(angle), -jnp.sin(angle)
    turns = lax.rem(cells[8:12].astype(jnp.int32) * me, NZ).astype(f32) * (2.0 * math.pi / NZ)
    first_re, first_im = jnp.cos(turns), jnp.sin(turns)
    gather(line_dst, None, 3, 3, GROUP - 1)

    def pick(i, state):
        p_re, p_im = state
        z = NZ - 1 - i
        x_re, x_im = line_dst[z, 0].astype(f32), line_dst[z, 1].astype(f32)
        return (
            p_re * w_re - p_im * w_im + x_re[None],
            p_re * w_im + p_im * w_re + x_im[None],
        )

    zero = jnp.zeros_like(w_re)
    p_re, p_im = lax.fori_loop(0, NZ, pick, (zero, zero), unroll=8)
    scale = 1.0 / math.sqrt(NZ)
    want = cells[0:8].reshape(4, 2, 16, 128)
    r_re = (want[:, 0] - p_re * scale) * scale
    r_im = (want[:, 1] - p_im * scale) * scale
    state = (r_re * first_re - r_im * first_im, r_re * first_im + r_im * first_re)

    def put(ref, z, state):
        t_re, t_im = state
        ref[z, 0] = (t_re[0] + t_re[1] + t_re[2] + t_re[3]).astype(bf16)
        ref[z, 1] = (t_im[0] + t_im[1] + t_im[2] + t_im[3]).astype(bf16)
        return (t_re * w_re + t_im * w_im, t_im * w_re - t_re * w_im)

    state = put(fix_dst, me, state)

    def expand(k, state):
        z, where = in_group(k)
        state = put(fix_src, z, state)
        remote(fix_src.at[z], fix_dst.at[me], send_sem.at[4], recv_sem.at[4], where).start()
        return state

    lax.fori_loop(1, GROUP, expand, state)

    gather(fix_dst, None, 4, 4, GROUP - 1)
    spread2[...] = fix_dst[...].reshape(GROUP * 32, 128).astype(f32)
    for c in range(4):
        at = slice(c * 256, c * 256 + 256)
        block = jnp.concatenate(
            [spread2[pl.ds(2 * c + k, 256, stride=8), :].astype(bf16) for k in range(2)], axis=1
        )
        res = dot(fine_t[...], block)
        real, imag = res[:256], res[256:]
        t_re, t_im = twist[0, :, at], twist[1, :, at]
        turned2[:, at] = (real * t_re + imag * t_im).astype(bf16)
        turned2[:, 1024 + c * 256 : 1280 + c * 256] = (imag * t_re - real * t_im).astype(bf16)
    for c in range(2):
        rows = pl.ds(pl.multiple_of((1 - plane) * HALF + c * 256, 256), 256)
        back_src[c] = dot(turned2[...], coarse[rows, :], NT).astype(bf16)
        remote(
            back_src.at[c], back_dst.at[c], pair_send.at[PARTS + c], pair_recv.at[PARTS + c],
            partner,
        ).start()
    for c in range(2):
        rows = pl.ds(pl.multiple_of(plane * HALF + c * 256, 256), 256)
        at = slice(c * 256, c * 256 + 256)
        blended[:, at] = guess[:, at] + dot(turned2[...], coarse[rows, :], NT)
    for c in range(2):
        at = slice(c * 256, c * 256 + 256)
        remote(
            back_src.at[c], back_dst.at[c], pair_send.at[PARTS + c], pair_recv.at[PARTS + c],
            partner,
        ).wait()
        blended[:, at] = blended[:, at] + back_dst[c].astype(f32)

    def send_columns(src, dst, which):
        @pl.loop(1, GROUP)
        def _(k):
            peer, where = in_group(k)
            remote(
                src.at[peer], dst.at[me], send_sem.at[which], recv_sem.at[which], where
            ).start()

    for q in range(4):
        for g in range(4):
            rows = [
                blended[q * 64 + r * 16 : q * 64 + r * 16 + 16, 128 * g : 128 * g + 128]
                for r in range(4)
            ]
            for i, block in enumerate(exchange_blocks(rows, 32)):
                high = block.astype(bf16)
                col_src[(4 * g + i) * 4 + q] = high
                rest_src[(4 * g + i) * 4 + q] = (block - high.astype(f32)).astype(bf16)
    send_columns(col_src, col_dst, 5)
    send_columns(rest_src, rest_dst, 6)
    col_dst[me] = col_src[me]
    rest_dst[me] = rest_src[me]

    for load in loads[13:]:
        load.wait()
    patch1[...] = dot(swap[...], patch1[...]).astype(bf16)
    unpatch1[...] = dot(unpatch1[...], swap[...]).astype(bf16)
    gather(col_dst, None, 5, 5, GROUP - 1)
    gain1 = gains.at[1]
    for zb in range(4):
        pix = col_dst[zb * 16 : zb * 16 + 16].reshape(256, 128)
        first = dot(pix, patch1[...], TN) + feat[...]
        for x in range(4):
            hidden[x * 128 + zb * 32 : x * 128 + zb * 32 + 32, :] = first[32 * x : 32 * x + 32, :]
    left1 = lax.broadcasted_iota(jnp.int32, (128, 128), 1) < 64

    @pl.loop(0, 4)
    def _(x):
        at = pl.ds(pl.multiple_of(128 * x, 128), 128)
        normed = norm(hidden[at, :], gain1[0:1, :])
        projected = dot(normed, qkv1[...]).astype(bf16)
        scaled = (projected[:, :D] * 0.125).astype(bf16)
        attended = attention(scaled, projected[:, D : 2 * D], projected[:, 2 * D :], left1)
        normed = tail(hidden[at, :], attended, out1, up1, down1, gain1)
        for zb in range(4):
            last[pl.ds(pl.multiple_of(zb * 128 + 32 * x, 32), 32), :] = normed[
                32 * zb : 32 * zb + 32, :
            ]

    gather(rest_dst, None, 6, 6, GROUP - 1)
    for j in range(4):
        rows = slice(128 * j, 128 * j + 128)
        moved = dot(deal[rows, :], last[...]).astype(bf16)
        value = scal[0] * dot(moved, unpatch1[...])
        for zb in range(4):
            for ref in (col_dst, rest_dst):
                pix = ref[zb * 16 : zb * 16 + 16].reshape(256, 128)
                value = value + dot(deal[rows, 128 * zb : 128 * zb + 128], pix, NT)
        final_src[2 * j : 2 * j + 2] = value.reshape(2, 64, 256)
    for peer, where in peers:
        remote(
            final_src.at[peer], final_dst.at[gy], send_sem.at[7], recv_sem.at[7], where
        ).start()
    final_dst[gy] = final_src[gy]

    def drain(src, which, count):
        part = pl.ds(0, count)
        pltpu.make_async_copy(src.at[part], src.at[part], send_sem.at[which]).wait()

    drain(own_src, 0, GY - 1)
    drain(oth_dst, 1, GY - 1)
    drain(relay_src, 2, GZ - 1)
    drain(line_src, 3, GROUP - 1)
    drain(fix_src, 4, GROUP - 1)
    drain(col_src, 5, GROUP - 1)
    drain(rest_src, 6, GROUP - 1)
    drain(final_src, 7, GY - 1)
    gather(relay_dst, None, 2, 2, GZ - 1)
    gather(final_dst, None, 7, 7, GY - 1)


def finish_kernel(coef, final, relay, noise, previous, estimate):
    row = lax.broadcasted_iota(jnp.int32, (8, 128), 0) < 4
    a, b, c = coef[0], coef[1], coef[2]
    for zb in range(4):
        for g in range(4):
            at = slice(8 * g, 8 * g + 8)
            for part in range(2):
                lanes = slice(128 * part, 128 * part + 128)
                blocks = []
                for yb in range(4):
                    base = 8 * ((zb * 4 + yb) // 2)
                    one = final[2 * g, base : base + 8, lanes]
                    two = final[2 * g + 1, base : base + 8, lanes]
                    if yb % 2 == 0:
                        blocks.append(jnp.where(row, one, pltpu.roll(two, 4, axis=0)))
                    else:
                        blocks.append(jnp.where(row, pltpu.roll(one, 4, axis=0), two))
                for i, block in enumerate(exchange_blocks(blocks, 16)):
                    for h in range(2):
                        z = zb * 16 + part * 8 + h * 4 + i
                        value = block[:, 64 * h : 64 * h + 64]
                        s = z % 4
                        old = relay[z // 4, at, 64 * s : 64 * s + 64]
                        estimate[z, at, :] = value
                        previous[z, at, :] = a * value + b * old + c * noise[z, at, :]


def local(
    noisy, noise, timestep, measured, cap_index, w_patch, w_qkv, w_out, w_up, w_down, w_unpatch,
    norm_gain,
):
    moment = timestep[0].astype(f32)
    signal_now = cumulative_alpha(moment)
    signal_prev = cumulative_alpha(moment - STRIDE)
    root_signal = jnp.sqrt(signal_now)
    root_noise = jnp.sqrt(1.0 - signal_now)
    features = time_features(moment)[None]
    scal = jnp.stack([root_noise, 1.0 / root_signal])
    toward = jnp.sqrt(
        (1.0 - signal_prev) * signal_now * (1.0 / signal_prev - 1.0) / (1.0 - signal_now)
    )
    spread = jnp.sqrt((1.0 - signal_prev) / (1.0 - signal_now) * (1.0 - signal_now / signal_prev))
    coef = jnp.stack(
        [jnp.sqrt(signal_prev) - toward * root_signal / root_noise, toward / root_noise, spread]
    )
    vmem = pl.BlockSpec(memory_space=pltpu.VMEM)
    smem = pl.BlockSpec(memory_space=pltpu.SMEM)
    anywhere = pl.BlockSpec(memory_space=pl.ANY)
    V = pltpu.VMEM
    weights = lambda: [
        V((PIX, D), bf16), V((D, 3 * D), bf16), V((D, D), bf16), V((D, FF), bf16),
        V((FF, D), bf16), V((D, PIX), bf16),
    ]
    final, relay = pl.pallas_call(
        step_kernel,
        out_shape=(
            jax.ShapeDtypeStruct((GY, 64, 256), f32),
            jax.ShapeDtypeStruct((GZ, 32, 256), f32),
        ),
        in_specs=[smem] + [vmem] * 5 + [anywhere] * 14,
        out_specs=(vmem, vmem),
        scratch_shapes=weights() + weights() + [
            V((1024, 2048), bf16), V((2, 256, 1024), f32), V((256, 512), bf16),
            V((512, 256), bf16), V((512, 512), bf16), V((256, 256), bf16),
            V((512, 512), bf16), V((512, 512), bf16),
            V((4, 256, 128), f32), V((12, 32, 128), f32),
            V((512, 512), bf16), V((GY, 64, 512), bf16), V((GY, 64, 512), bf16),
            V((GY, 64, 256), bf16), V((GZ, 32, 256), f32),
            V((HALF, PIX), bf16), V((HALF, PIX), bf16), V((HALF, D), f32), V((HALF, D), bf16),
            V((2 * HALF, 2 * D), bf16), V((PIX, HALF), f32), V((PARTS, PIX, CHUNK), bf16),
            V((PARTS, PIX, CHUNK), bf16),
            V((PIX, 2048), f32), V((512, 1024), bf16), V((512, 128), f32),
            V((GROUP, 2, 16, 128), bf16), V((GROUP, 2, 16, 128), bf16),
            V((12, 16, 128), f32), V((GROUP, 2, 16, 128), bf16), V((GROUP, 2, 16, 128), bf16),
            V((PIX, 2048), bf16), V((GROUP * 32, 128), f32), V((2, PIX, 256), bf16),
            V((2, PIX, 256), bf16), V((PIX, HALF), f32),
            V((GROUP, 16, 128), bf16), V((GROUP, 16, 128), bf16),
            V((GROUP, 16, 128), bf16), V((GROUP, 16, 128), bf16),
            V((512, D), bf16), V((GY, 64, 256), f32),
            pltpu.SemaphoreType.DMA((20,)), pltpu.SemaphoreType.DMA((8,)),
            pltpu.SemaphoreType.DMA((8,)), pltpu.SemaphoreType.DMA((PARTS + 2,)),
            pltpu.SemaphoreType.DMA((PARTS + 2,)),
        ],
        compiler_params=pltpu.CompilerParams(
            collective_id=0, has_side_effects=True, vmem_limit_bytes=56 * MIB
        ),
    )(
        scal, features, norm_gain, noisy.reshape(256, LAT), measured.reshape(8, 32, 64), cap_index,
        w_patch, w_qkv, w_out, w_up, w_down, w_unpatch, *(jnp.asarray(t) for t in tables()),
    )
    shape = jax.ShapeDtypeStruct((NZ, 32, 64), f32)
    previous, estimate = pl.pallas_call(
        finish_kernel,
        out_shape=(shape, shape),
        in_specs=[smem] + [vmem] * 3,
        out_specs=(vmem, vmem),
        compiler_params=pltpu.CompilerParams(vmem_limit_bytes=32 * MIB),
    )(coef, final, relay, noise.transpose(0, 2, 1))
    return (previous.transpose(0, 2, 1), estimate.transpose(0, 2, 1))


def solution(mesh):
    placed = (
        P("gz", "gy", None),
        P(None, "gy", "gz"),
        P(),
        P(None, None, "gz", "gy"),
        P(None, "gz", "gy"),
    ) + (P(),) * 7
    return jax.shard_map(
        local,
        mesh=mesh,
        in_specs=placed,
        out_specs=(P(None, "gy", "gz"), P(None, "gy", "gz")),
        check_vma=False,
    )
```

```python
import math

import jax
import jax.numpy as jnp
import numpy as np
from jax import lax
from jax.experimental import pallas as pl
from jax.experimental.pallas import tpu as pltpu
from jax.sharding import PartitionSpec as P

PATCH = 16
D = 384
HEADS = 6
FF = 1536
TRAIN_STEPS = 1000
STRIDE = 100
NZ = 64
LAT = 512
GZ = 16
GY = 8
NY = 4
GROUP = GZ * NY
SIDE = LAT // PATCH
HALF = SIDE * SIDE // 2
PIX = PATCH * PATCH
norm_eps = 1e-05
MIB = 1024 * 1024
f32 = jnp.float32
bf16 = jnp.bfloat16
MESH_ID = pl.DeviceIdType.MESH
NT = (((1,), (1,)), ((), ()))
TN = (((0,), (0,)), ((), ()))


def tables():
    parity, half_x, block_y = np.meshgrid(np.arange(2), np.arange(16), np.arange(32), indexing="ij")
    block_x = (2 * half_x + parity).reshape(-1)
    block_y = block_y.reshape(-1)
    by, bx = np.meshgrid(np.arange(32), np.arange(32), indexing="ij")
    by, bx = by.reshape(-1), bx.reshape(-1)
    turn = 2 * np.pi * ((block_y[:, None] * by[None] + block_x[:, None] * bx[None]) % 32) / 32
    coarse = np.concatenate([np.cos(turn), -np.sin(turn)], axis=1)
    xi, yi = np.meshgrid(np.arange(16), np.arange(16), indexing="ij")
    xi, yi = xi.reshape(-1), yi.reshape(-1)
    turn = 2 * np.pi * ((yi[:, None] * by[None] + xi[:, None] * bx[None]) % 512) / 512
    twist = np.stack([np.cos(turn), -np.sin(turn)]) / 32.0
    fine = np.zeros((2, 16, 4, 2, 2, 2, 256))
    for half in range(2):
        for quarter in range(4):
            for rest in range(2):
                ax = 8 * half + 2 * quarter + rest
                turn = 2 * np.pi * ((np.arange(16)[:, None] * yi[None] + ax * xi[None]) % 16) / 16
                fine[half, :, quarter, 0, rest, 0] = np.cos(turn)
                fine[half, :, quarter, 0, rest, 1] = np.sin(turn)
                fine[half, :, quarter, 1, rest, 0] = -np.sin(turn)
                fine[half, :, quarter, 1, rest, 1] = np.cos(turn)
    fine = fine.reshape(2, 256, 512) / 16.0
    to_bf = lambda a: a.astype(jnp.bfloat16)
    order = np.zeros((512, 512), np.float32)
    for gy in range(8):
        for hx in range(16):
            for yb in range(4):
                order[hx * 32 + gy * 4 + yb, gy * 64 + hx * 4 + yb] = 1.0
    swap = np.zeros((256, 256), np.float32)
    for y in range(16):
        for x in range(16):
            swap[x * 16 + y, y * 16 + x] = 1.0
    cast = np.zeros((512, 512), np.float32)
    for xb in range(32):
        for s in range(4):
            for yb in range(4):
                cast[(xb % 2) * 256 + s * 64 + (xb // 2) * 4 + yb, xb * 16 + s * 4 + yb] = 1.0
    deal = np.zeros((256, 256), np.float32)
    spill = np.zeros((2, 256, 512), np.float32)
    for x in range(4):
        for zb in range(4):
            for yb in range(32):
                row = (yb // 4) * 32 + (x % 2) * 16 + zb * 4 + yb % 4
                deal[row, (x % 2) * 128 + zb * 32 + yb] = 1.0
                spill[x // 2, row, zb * 128 + x * 32 + yb] = 1.0
    return (
        to_bf(coarse),
        twist.astype(np.float32),
        to_bf(fine),
        to_bf(np.ascontiguousarray(fine.transpose(0, 2, 1))),
        to_bf(order),
        to_bf(swap),
        to_bf(cast),
        to_bf(deal),
        to_bf(spill),
    )


def cumulative_alpha(moment):
    phase_angle = (moment / TRAIN_STEPS + 0.008) / 1.008 * (math.pi / 2.0)
    return jnp.cos(phase_angle) ** 2


def time_features(moment):
    half_width = D // 2
    frequency = jnp.exp(
        -math.log(10000.0) * jnp.arange(half_width).astype(jnp.float32) / half_width
    )
    angles = moment * frequency
    return jnp.concatenate([jnp.sin(angles), jnp.cos(angles)])


def dot(a, b, dims=None):
    if dims is None:
        return jnp.dot(a, b, preferred_element_type=f32)
    return lax.dot_general(a, b, dims, preferred_element_type=f32)


def norm(values, gain_row):
    average = jnp.mean(values, axis=-1, keepdims=True)
    centred = values - average
    variance = jnp.mean(centred * centred, axis=-1, keepdims=True)
    return (centred * lax.rsqrt(variance + norm_eps) * gain_row).astype(bf16)


def gelu(v):
    return 0.5 * v * (1.0 + jnp.tanh(math.sqrt(2.0 / math.pi) * (v + 0.044715 * (v * v * v))))


def exchange_blocks(arrays, width):
    arrays = list(arrays)
    lane = lax.broadcasted_iota(jnp.int32, arrays[0].shape, 1) // width
    step = 1
    while step < len(arrays):
        low = (lane // step) % 2 == 0
        for i in range(len(arrays)):
            if i & step == 0:
                a, b = arrays[i], arrays[i | step]
                arrays[i] = jnp.where(low, a, pltpu.roll(b, step * width, axis=1))
                arrays[i | step] = jnp.where(low, pltpu.roll(a, 128 - step * width, axis=1), b)
        step *= 2
    return arrays


def attention(queries, keys, values, left):
    outs = []
    for pair in range(HEADS // 2):
        lanes = slice(128 * pair, 128 * pair + 128)
        q, k, v = queries[:, lanes], keys[:, lanes], values[:, lanes]
        halves = []
        for which in range(2):
            q_one = jnp.where(left if which == 0 else ~left, q, jnp.zeros_like(q))
            scores = dot(q_one, k, NT)
            top = jnp.max(scores, axis=-1, keepdims=True)
            raised = jnp.exp(scores - top)
            total = jnp.sum(raised, axis=-1, keepdims=True)
            halves.append(dot(raised.astype(bf16), v) / total)
        outs.append(jnp.where(left, halves[0], halves[1]).astype(bf16))
    return jnp.concatenate(outs, axis=1)


def tail(hidden, attended, w_out, w_up, w_down, gain1, gain2):
    hidden = hidden + dot(attended, w_out[...])
    inner = gelu(dot(norm(hidden, gain1), w_up[...])).astype(bf16)
    hidden = hidden + dot(inner, w_down[...])
    return norm(hidden, gain2)


PARTS = 4
CHUNK = HALF // PARTS


def step_kernel(*refs):
    (
        consts, gains, noisy, noise, measured, cap,
        h_patch, h_qkv, h_out, h_up, h_down, h_unpatch,
        h_coarse, h_twist, h_fine, h_fine_t, h_order, h_swap, h_cast, h_deal, h_spill,
        previous, estimate,
        patch0, qkv0, out0, up0, down0, unpatch0,
        patch1, qkv1, out1, up1, down1, unpatch1,
        coarse, twist, fine, fine_t, order, swap, cast, deal, spill,
        strips, wide, cut, high_src, low_src, own_dst, oth_dst, low_dst, relay_src, relay_dst,
        tok, hidden, queries, pairs, guess, guess16, guess_dst,
        summed, turned, spread, line_src, line_dst,
        cells, fix_src, fix_dst, turned2, spread2, back_src, back_dst, blended,
        col_src, col_dst, final_src, final_dst,
        load_sem, send_sem, recv_sem, pair_send, pair_recv, ready,
    ) = refs
    gz, gy = lax.axis_index("gz"), lax.axis_index("gy")
    plane, y = gy // NY, gy % NY
    me = gz * NY + y
    feat = consts[0:1, :]
    root_noise, inv_signal = consts[1:2, 0:1], consts[1:2, 1:2]

    plan = [
        (h_cast, cast), (h_swap, swap), (h_order, order), (h_patch.at[0], patch0),
        (h_qkv.at[0], qkv0), (h_out.at[0], out0), (h_up.at[0], up0), (h_down.at[0], down0),
        (h_unpatch.at[0], unpatch0), (h_coarse, coarse), (h_twist, twist),
        (h_fine.at[plane], fine), (h_fine_t.at[plane], fine_t),
        (h_patch.at[1], patch1), (h_qkv.at[1], qkv1), (h_out.at[1], out1), (h_up.at[1], up1),
        (h_down.at[1], down1), (h_unpatch.at[1], unpatch1), (h_deal, deal),
        (h_spill, spill),
    ]
    loads = [
        pltpu.make_async_copy(src, dst, load_sem.at[i]) for i, (src, dst) in enumerate(plan)
    ]
    for load in loads:
        load.start()

    def in_group(k):
        peer = lax.rem(me + k, GROUP)
        return peer, {"gz": peer // NY, "gy": plane * NY + lax.rem(peer, NY)}

    def in_other_plane(k):
        return {"gy": (1 - plane) * NY + lax.rem(y + k, NY)}

    barrier = pltpu.get_barrier_semaphore()
    for k in range(1, GY):
        pl.semaphore_signal(
            barrier, inc=1, device_id={"gy": lax.rem(gy + k, GY)}, device_id_type=MESH_ID
        )
    for k in range(1, GZ):
        pl.semaphore_signal(
            barrier, inc=1, device_id={"gz": lax.rem(gz + k, GZ)}, device_id_type=MESH_ID
        )

    def remote(src, dst, send, recv, where):
        return pltpu.make_async_remote_copy(
            src_ref=src, dst_ref=dst, send_sem=send, recv_sem=recv,
            device_id=where, device_id_type=MESH_ID,
        )

    for g in range(4):
        strips[g] = noisy[:, 128 * g : 128 * g + 128]
        for part in range(2):
            rows = [strips[g, pl.ds(8 * part + i, 16, stride=16), :] for i in range(8)]
            for i, block in enumerate(exchange_blocks(rows, 16)):
                high = block.astype(bf16)
                at = slice((8 * g + i) * 16, (8 * g + i) * 16 + 16)
                cut[at, 128 * part : 128 * part + 128] = high
                cut[at, 256 + 128 * part : 384 + 128 * part] = (
                    block - high.astype(f32)
                ).astype(bf16)
    loads[0].wait()
    sorted_rows = dot(cast[...], cut[...]).astype(bf16).reshape(GY, 64, 512)
    high_src[...] = sorted_rows[:, :, :256]
    low_src[...] = sorted_rows[:, :, 256:]

    pl.semaphore_wait(barrier, GY - 1 + GZ - 1)
    peers = []
    for k in range(1, GY):
        peer = lax.rem(gy + k, GY)
        where = {"gy": peer}
        flip = lax.rem(peer + NY, GY)
        peers.append((peer, where))
        remote(high_src.at[flip], oth_dst.at[gy], send_sem.at[1], recv_sem.at[1], where).start()
        remote(high_src.at[peer], own_dst.at[gy], send_sem.at[0], recv_sem.at[0], where).start()
    for peer, where in peers:
        remote(low_src.at[peer], low_dst.at[gy], send_sem.at[6], recv_sem.at[6], where).start()
    for k in range(1, NY):
        pl.semaphore_signal(
            ready, inc=1, device_id={"gy": plane * NY + lax.rem(y + k, NY)},
            device_id_type=MESH_ID,
        )
    own_dst[gy] = high_src[gy]
    oth_dst[gy] = high_src[lax.rem(gy + NY, GY)]
    low_dst[gy] = low_src[gy]

    for s in range(2):
        for g in range(4):
            part = noisy[128 * s : 128 * s + 128, 128 * g : 128 * g + 128].T
            relay_src[4 * g : 4 * g + 4, :, 128 * s : 128 * s + 128] = part.reshape(4, 32, 128)

    @pl.loop(1, GZ)
    def _(k):
        peer = lax.rem(gz + k, GZ)
        remote(
            relay_src.at[peer], relay_dst.at[gz], send_sem.at[2], recv_sem.at[2], {"gz": peer}
        ).start()

    relay_dst[gz] = relay_src[gz]

    for a in range(12):
        wide[a, :, 0:64] = measured[a] if a < 8 else cap[a - 8].astype(f32)
        quarter = [wide[a, pl.ds(q, 8, stride=4), :] for q in range(4)]
        for r in range(2):
            cells[a, 8 * r : 8 * r + 8, :] = jnp.concatenate(
                [v[:, 32 * r : 32 * r + 32] for v in quarter], axis=1
            )

    for load in loads[1:9]:
        load.wait()
    unpatch0[...] = dot(unpatch0[...], swap[...]).astype(bf16)

    def gather(dst, src, s, r, count):
        part = pl.ds(0, count)
        del src
        pltpu.make_async_copy(dst.at[part], dst.at[part], recv_sem.at[r]).wait()

    gather(own_dst, None, 0, 0, GY - 1)
    gather(oth_dst, None, 1, 1, GY - 1)
    tok[...] = dot(order[...], own_dst[...].reshape(HALF, 256)).astype(bf16)

    def gain(m, r):
        return gains[r, m : m + 1, :]

    first = dot(tok[...], patch0[...]) + feat
    hidden[...] = first
    normed = norm(first, gain(0, 0))
    queries[...] = (dot(normed, qkv0[:, :D]).astype(bf16) * 0.125).astype(bf16)
    pairs[0:HALF, :] = dot(normed, qkv0[:, D:]).astype(bf16)
    normed = norm(dot(oth_dst[...].reshape(HALF, 256), patch0[...]) + feat, gain(0, 0))
    pairs[HALF:, :] = dot(normed, qkv0[:, D:]).astype(bf16)

    partner = {"gy": (1 - plane) * NY + y}
    left = lax.broadcasted_iota(jnp.int32, (HALF, 128), 1) < 64
    attended = attention(queries[...], pairs[:, :D], pairs[:, D:], left)
    queries[...] = tail(hidden[...], attended, out0, up0, down0, gain(0, 1), gain(0, 2))
    gather(low_dst, None, 6, 6, GY - 1)
    low = dot(order[...], low_dst[...].reshape(HALF, 256)).astype(bf16)
    summed[:, 0:HALF] = dot(swap[...], tok[...], NT) + dot(swap[...], low, NT)
    for i in range(PARTS):
        at = slice(i * CHUNK, i * CHUNK + CHUNK)
        net = dot(unpatch0[...], queries[at, :], (((0,), (1,)), ((), ())))
        first = (summed[:, at] - root_noise * net) * inv_signal
        guess[:, at] = first
        guess16[i] = first.astype(bf16)
        remote(
            guess16.at[i], guess_dst.at[i], pair_send.at[i], pair_recv.at[i], partner
        ).start()

    for load in loads[9:13]:
        load.wait()
    half_rows = pl.ds(pl.multiple_of(plane * HALF, HALF), HALF)
    side_rows = pl.ds(pl.multiple_of((1 - plane) * HALF, HALF), HALF)
    mine = jnp.concatenate([guess16[i] for i in range(PARTS)], axis=1)
    for c in range(4):
        at = slice(512 * c, 512 * c + 512)
        summed[:, at] = dot(mine, coarse[half_rows, at])
    for i in range(PARTS):
        remote(
            guess16.at[i], guess_dst.at[i], pair_send.at[i], pair_recv.at[i], partner
        ).wait()
    theirs = jnp.concatenate([guess_dst[i] for i in range(PARTS)], axis=1)
    for c in range(4):
        at = slice(256 * c, 256 * c + 256)
        im = slice(1024 + 256 * c, 1280 + 256 * c)
        real = summed[:, at] + dot(theirs, coarse[side_rows, at])
        imag = summed[:, im] + dot(theirs, coarse[side_rows, im])
        t_re, t_im = twist[0, :, at], twist[1, :, at]
        turned[0:256, at] = (real * t_re - imag * t_im).astype(bf16)
        turned[256:512, at] = (real * t_im + imag * t_re).astype(bf16)

    pl.semaphore_wait(ready, NY - 1)

    @pl.loop(0, 4)
    def _(i):
        block = lax.rem(i + gz // 4, 4)
        res = dot(fine[pl.ds(pl.multiple_of(block * 64, 64), 64), :], turned[...])
        for c in range(8):
            spread[pl.ds(c, 64, stride=8), :] = res[:, 128 * c : 128 * c + 128]
        line_src[pl.ds(block * 16, 16)] = spread[...].astype(bf16).reshape(16, 2, 16, 128)

        @pl.loop(0, 16)
        def _(j):
            peer = block * 16 + j

            @pl.when(peer != me)
            def _():
                where = {"gz": peer // NY, "gy": plane * NY + lax.rem(peer, NY)}
                remote(
                    line_src.at[peer], line_dst.at[me], send_sem.at[3], recv_sem.at[3], where
                ).start()

    line_dst[me] = line_src[me]

    angle = cells[8:12] * (2.0 * math.pi / NZ)
    w_re, w_im = jnp.cos(angle), -jnp.sin(angle)
    turns = lax.rem(cells[8:12].astype(jnp.int32) * me, NZ).astype(f32) * (2.0 * math.pi / NZ)
    first_re, first_im = jnp.cos(turns), jnp.sin(turns)
    gather(line_dst, None, 3, 3, GROUP - 1)

    def pick(i, state):
        p_re, p_im = state
        z = NZ - 1 - i
        x_re, x_im = line_dst[z, 0].astype(f32), line_dst[z, 1].astype(f32)
        return (
            p_re * w_re - p_im * w_im + x_re[None],
            p_re * w_im + p_im * w_re + x_im[None],
        )

    zero = jnp.zeros_like(w_re)
    p_re, p_im = lax.fori_loop(0, NZ, pick, (zero, zero), unroll=8)
    scale = 1.0 / math.sqrt(NZ)
    want = cells[0:8].reshape(4, 2, 16, 128)
    r_re = (want[:, 0] - p_re * scale) * scale
    r_im = (want[:, 1] - p_im * scale) * scale
    state = (r_re * first_re - r_im * first_im, r_re * first_im + r_im * first_re)

    def put(ref, z, state):
        t_re, t_im = state
        ref[z, 0] = (t_re[0] + t_re[1] + t_re[2] + t_re[3]).astype(bf16)
        ref[z, 1] = (t_im[0] + t_im[1] + t_im[2] + t_im[3]).astype(bf16)
        return (t_re * w_re + t_im * w_im, t_im * w_re - t_re * w_im)

    state = put(fix_dst, me, state)

    def expand(k, state):
        z, where = in_group(k)
        state = put(fix_src, z, state)
        remote(fix_src.at[z], fix_dst.at[me], send_sem.at[4], recv_sem.at[4], where).start()
        return state

    lax.fori_loop(1, GROUP, expand, state)

    gather(fix_dst, None, 4, 4, GROUP - 1)
    spread2[...] = fix_dst[...].reshape(GROUP * 32, 128).astype(f32)
    for c in range(4):
        at = slice(c * 256, c * 256 + 256)
        block = jnp.concatenate(
            [spread2[pl.ds(2 * c + k, 256, stride=8), :].astype(bf16) for k in range(2)], axis=1
        )
        res = dot(fine_t[...], block)
        real, imag = res[:256], res[256:]
        t_re, t_im = twist[0, :, at], twist[1, :, at]
        turned2[:, at] = (real * t_re + imag * t_im).astype(bf16)
        turned2[:, 1024 + c * 256 : 1280 + c * 256] = (imag * t_re - real * t_im).astype(bf16)
    for c in range(2):
        rows = pl.ds(pl.multiple_of((1 - plane) * HALF + c * 256, 256), 256)
        back_src[c] = dot(turned2[...], coarse[rows, :], NT).astype(bf16)
        remote(
            back_src.at[c], back_dst.at[c], pair_send.at[PARTS + c], pair_recv.at[PARTS + c],
            partner,
        ).start()
    for c in range(2):
        rows = pl.ds(pl.multiple_of(plane * HALF + c * 256, 256), 256)
        at = slice(c * 256, c * 256 + 256)
        blended[:, at] = guess[:, at] + dot(turned2[...], coarse[rows, :], NT)
    for c in range(2):
        at = slice(c * 256, c * 256 + 256)
        remote(
            back_src.at[c], back_dst.at[c], pair_send.at[PARTS + c], pair_recv.at[PARTS + c],
            partner,
        ).wait()
        blended[:, at] = blended[:, at] + back_dst[c].astype(f32)

    for q in range(4):
        for g in range(4):
            rows = [
                blended[q * 64 + r * 16 : q * 64 + r * 16 + 16, 128 * g : 128 * g + 128]
                for r in range(4)
            ]
            for i, block in enumerate(exchange_blocks(rows, 32)):
                col_src[(4 * g + i) * 4 + q] = block.astype(bf16)

    @pl.loop(1, GROUP)
    def _(k):
        peer, where = in_group(k)
        remote(col_src.at[peer], col_dst.at[me], send_sem.at[5], recv_sem.at[5], where).start()

    col_dst[me] = col_src[me]

    gather(relay_dst, None, 2, 2, GZ - 1)
    c_est, c_old, c_new = consts[1:2, 2:3], consts[1:2, 3:4], consts[1:2, 4:5]

    @pl.loop(0, GZ)
    def _(i):
        for z in range(4):
            previous[4 * i + z] = (
                c_old * relay_dst[i, :, 64 * z : 64 * z + 64] + c_new * noise[4 * i + z]
            )

    for load in loads[13:]:
        load.wait()
    patch1[...] = dot(swap[...], patch1[...]).astype(bf16)
    unpatch1[...] = dot(unpatch1[...], swap[...]).astype(bf16)
    gather(col_dst, None, 5, 5, GROUP - 1)
    for zb in range(4):
        pix = col_dst[zb * 16 : zb * 16 + 16].reshape(256, 128)
        first = dot(pix, patch1[...], TN) + feat
        for x in range(4):
            hidden[x * 128 + zb * 32 : x * 128 + zb * 32 + 32, :] = first[32 * x : 32 * x + 32, :]
    normed = norm(hidden[...], gain(1, 0))
    queries[...] = (dot(normed, qkv1[:, :D]).astype(bf16) * 0.125).astype(bf16)
    pairs[0:HALF, :] = dot(normed, qkv1[:, D:]).astype(bf16)
    left1 = lax.broadcasted_iota(jnp.int32, (128, 128), 1) < 64
    for p in range(2):
        half = slice(256 * p, 256 * p + 256)
        attended = []
        for x in range(2):
            at = slice(256 * p + 128 * x, 256 * p + 128 * x + 128)
            attended.append(attention(queries[at, :], pairs[at, :D], pairs[at, D:], left1))
        attended = jnp.concatenate(attended, axis=0)
        normed = tail(hidden[half, :], attended, out1, up1, down1, gain(1, 1), gain(1, 2))
        moved = dot(deal[...], normed).astype(bf16)
        value = root_noise * dot(moved, unpatch1[...])
        for zb in range(4):
            pix = col_dst[zb * 16 : zb * 16 + 16].reshape(256, 128)
            value = value + dot(spill[p, :, 128 * zb : 128 * zb + 128], pix, NT)
        for h in range(2):
            final_src[p, :, h] = value[:, 128 * h : 128 * h + 128].reshape(GY, 32, 128)
        here = pl.ds(pl.multiple_of(gy * 64 + p * 32, 32), 32)
        for peer, where in peers:
            remote(
                final_src.at[p, peer], final_dst.at[:, here, :], send_sem.at[7], recv_sem.at[7],
                where,
            ).start()
        final_dst[:, here, :] = final_src[p, gy]

    def drain(src, which, count):
        part = pl.ds(0, count)
        pltpu.make_async_copy(src.at[part], src.at[part], send_sem.at[which]).wait()

    drain(high_src, 0, GY - 1)
    drain(high_src, 1, GY - 1)
    drain(low_src, 6, GY - 1)
    drain(relay_src, 2, GZ - 1)
    drain(line_src, 3, GROUP - 1)
    drain(fix_src, 4, GROUP - 1)
    drain(col_src, 5, GROUP - 1)
    done = final_dst.at[:, pl.ds(0, (GY - 1) * 64), :]
    pltpu.make_async_copy(done, done, send_sem.at[7]).wait()
    pltpu.make_async_copy(done, done, recv_sem.at[7]).wait()

    for g in range(4):
        at = slice(8 * g, 8 * g + 8)
        for zb in range(4):
            for h in range(2):
                blocks = [
                    final_dst[h, pl.ds(128 * g + zb * 4 + yb, 8, stride=16), :] for yb in range(4)
                ]
                for i, block in enumerate(exchange_blocks(blocks, 16)):
                    for part in range(2):
                        z = zb * 16 + h * 8 + part * 4 + i
                        value = block[:, 64 * part : 64 * part + 64]
                        estimate[z, at, :] = value
                        previous[z, at, :] = previous[z, at, :] + c_est * value


def local(
    noisy, noise, timestep, measured, cap_index, w_patch, w_qkv, w_out, w_up, w_down, w_unpatch,
    norm_gain,
):
    moment = timestep[0].astype(f32)
    signal_now = cumulative_alpha(moment)
    signal_prev = cumulative_alpha(moment - STRIDE)
    root_signal = jnp.sqrt(signal_now)
    root_noise = jnp.sqrt(1.0 - signal_now)
    toward = jnp.sqrt(
        (1.0 - signal_prev) * signal_now * (1.0 / signal_prev - 1.0) / (1.0 - signal_now)
    )
    spread = jnp.sqrt((1.0 - signal_prev) / (1.0 - signal_now) * (1.0 - signal_now / signal_prev))
    coefs = (
        root_noise, 1.0 / root_signal, jnp.sqrt(signal_prev) - toward * root_signal / root_noise,
        toward / root_noise, spread,
    )
    place = lax.broadcasted_iota(jnp.int32, (1, D), 1)
    row = jnp.zeros((1, D), f32)
    for i, value in enumerate(coefs):
        row = jnp.where(place == i, value, row)
    consts = jnp.concatenate([time_features(moment)[None], row], axis=0)
    vmem = pl.BlockSpec(memory_space=pltpu.VMEM)
    anywhere = pl.BlockSpec(memory_space=pl.ANY)
    V = pltpu.VMEM
    weights = lambda: [
        V((PIX, D), bf16), V((D, 3 * D), bf16), V((D, D), bf16), V((D, FF), bf16),
        V((FF, D), bf16), V((D, PIX), bf16),
    ]
    shape = jax.ShapeDtypeStruct((NZ, 32, 64), f32)
    previous, estimate = pl.pallas_call(
        step_kernel,
        out_shape=(shape, shape),
        in_specs=[vmem] * 6 + [anywhere] * 15,
        out_specs=(vmem, vmem),
        scratch_shapes=weights() + weights() + [
            V((1024, 2048), bf16), V((2, 256, 1024), f32), V((256, 512), bf16),
            V((512, 256), bf16), V((512, 512), bf16), V((256, 256), bf16),
            V((512, 512), bf16), V((256, 256), bf16), V((2, 256, 512), bf16),
            V((4, 256, 128), f32), V((12, 32, 128), f32), V((512, 512), bf16),
            V((GY, 64, 256), bf16), V((GY, 64, 256), bf16), V((GY, 64, 256), bf16),
            V((GY, 64, 256), bf16), V((GY, 64, 256), bf16),
            V((GZ, 32, 256), f32), V((GZ, 32, 256), f32),
            V((HALF, PIX), bf16), V((HALF, D), f32), V((HALF, D), bf16),
            V((2 * HALF, 2 * D), bf16), V((PIX, HALF), f32), V((PARTS, PIX, CHUNK), bf16),
            V((PARTS, PIX, CHUNK), bf16),
            V((PIX, 2048), f32), V((512, 1024), bf16), V((512, 128), f32),
            V((GROUP, 2, 16, 128), bf16), V((GROUP, 2, 16, 128), bf16),
            V((12, 16, 128), f32), V((GROUP, 2, 16, 128), bf16), V((GROUP, 2, 16, 128), bf16),
            V((PIX, 2048), bf16), V((GROUP * 32, 128), f32), V((2, PIX, 256), bf16),
            V((2, PIX, 256), bf16), V((PIX, HALF), f32),
            V((GROUP, 16, 128), bf16), V((GROUP, 16, 128), bf16),
            V((2, GY, 2, 32, 128), f32), V((2, 512, 128), f32),
            pltpu.SemaphoreType.DMA((21,)), pltpu.SemaphoreType.DMA((8,)),
            pltpu.SemaphoreType.DMA((8,)), pltpu.SemaphoreType.DMA((PARTS + 2,)),
            pltpu.SemaphoreType.DMA((PARTS + 2,)), pltpu.SemaphoreType.REGULAR,
        ],
        compiler_params=pltpu.CompilerParams(
            collective_id=0, has_side_effects=True, vmem_limit_bytes=58 * MIB
        ),
    )(
        consts, norm_gain.transpose(1, 0, 2), noisy.reshape(256, LAT), noise.transpose(0, 2, 1),
        measured.reshape(8, 32, 64), cap_index,
        w_patch, w_qkv, w_out, w_up, w_down, w_unpatch, *(jnp.asarray(t) for t in tables()),
    )
    return (previous.transpose(0, 2, 1), estimate.transpose(0, 2, 1))


def solution(mesh):
    placed = (
        P("gz", "gy", None),
        P(None, "gy", "gz"),
        P(),
        P(None, None, "gz", "gy"),
        P(None, "gz", "gy"),
    ) + (P(),) * 7
    return jax.shard_map(
        local,
        mesh=mesh,
        in_specs=placed,
        out_specs=(P(None, "gy", "gz"), P(None, "gy", "gz")),
        check_vma=False,
    )
```

```python
import math

import jax
import jax.numpy as jnp
import numpy as np
from jax import lax
from jax.experimental import pallas as pl
from jax.experimental.pallas import tpu as pltpu
from jax.sharding import PartitionSpec as P

PATCH = 16
D = 384
HEADS = 6
FF = 1536
TRAIN_STEPS = 1000
STRIDE = 100
NZ = 64
LAT = 512
GZ = 16
GY = 8
NY = 4
GROUP = GZ * NY
SIDE = LAT // PATCH
HALF = SIDE * SIDE // 2
PIX = PATCH * PATCH
norm_eps = 1e-05
MIB = 1024 * 1024
f32 = jnp.float32
bf16 = jnp.bfloat16
MESH_ID = pl.DeviceIdType.MESH
NT = (((1,), (1,)), ((), ()))
TN = (((0,), (0,)), ((), ()))


def tables():
    parity, half_x, block_y = np.meshgrid(np.arange(2), np.arange(16), np.arange(32), indexing="ij")
    block_x = (2 * half_x + parity).reshape(-1)
    block_y = block_y.reshape(-1)
    by, bx = np.meshgrid(np.arange(32), np.arange(32), indexing="ij")
    by, bx = by.reshape(-1), bx.reshape(-1)
    turn = 2 * np.pi * ((block_y[:, None] * by[None] + block_x[:, None] * bx[None]) % 32) / 32
    coarse = np.concatenate([np.cos(turn), -np.sin(turn)], axis=1)
    xi, yi = np.meshgrid(np.arange(16), np.arange(16), indexing="ij")
    xi, yi = xi.reshape(-1), yi.reshape(-1)
    turn = 2 * np.pi * ((yi[:, None] * by[None] + xi[:, None] * bx[None]) % 512) / 512
    twist = np.stack([np.cos(turn), -np.sin(turn)]) / 32.0
    fine = np.zeros((2, 16, 4, 2, 2, 2, 256))
    for half in range(2):
        for quarter in range(4):
            for rest in range(2):
                ax = 8 * half + 2 * quarter + rest
                turn = 2 * np.pi * ((np.arange(16)[:, None] * yi[None] + ax * xi[None]) % 16) / 16
                fine[half, :, quarter, 0, rest, 0] = np.cos(turn)
                fine[half, :, quarter, 0, rest, 1] = np.sin(turn)
                fine[half, :, quarter, 1, rest, 0] = -np.sin(turn)
                fine[half, :, quarter, 1, rest, 1] = np.cos(turn)
    fine = fine.reshape(2, 256, 512) / 16.0
    to_bf = lambda a: a.astype(jnp.bfloat16)
    order = np.zeros((512, 512), np.float32)
    for gy in range(8):
        for hx in range(16):
            for yb in range(4):
                order[hx * 32 + gy * 4 + yb, gy * 64 + hx * 4 + yb] = 1.0
    swap = np.zeros((256, 256), np.float32)
    for y in range(16):
        for x in range(16):
            swap[x * 16 + y, y * 16 + x] = 1.0
    cast = np.zeros((512, 512), np.float32)
    for xb in range(32):
        for s in range(4):
            for yb in range(4):
                cast[(xb % 2) * 256 + s * 64 + (xb // 2) * 4 + yb, xb * 16 + s * 4 + yb] = 1.0
    deal = np.zeros((256, 256), np.float32)
    spill = np.zeros((2, 256, 512), np.float32)
    for x in range(4):
        for zb in range(4):
            for yb in range(32):
                row = (yb // 4) * 32 + (x % 2) * 16 + zb * 4 + yb % 4
                deal[row, (x % 2) * 128 + zb * 32 + yb] = 1.0
                spill[x // 2, row, zb * 128 + x * 32 + yb] = 1.0
    return (
        to_bf(coarse),
        twist.astype(np.float32),
        to_bf(fine),
        to_bf(np.ascontiguousarray(fine.transpose(0, 2, 1))),
        to_bf(order),
        to_bf(swap),
        to_bf(cast),
        to_bf(deal),
        to_bf(spill),
    )


def cumulative_alpha(moment):
    phase_angle = (moment / TRAIN_STEPS + 0.008) / 1.008 * (math.pi / 2.0)
    return jnp.cos(phase_angle) ** 2


def time_features(moment):
    half_width = D // 2
    frequency = jnp.exp(
        -math.log(10000.0) * jnp.arange(half_width).astype(jnp.float32) / half_width
    )
    angles = moment * frequency
    return jnp.concatenate([jnp.sin(angles), jnp.cos(angles)])


def dot(a, b, dims=None):
    if dims is None:
        return jnp.dot(a, b, preferred_element_type=f32)
    return lax.dot_general(a, b, dims, preferred_element_type=f32)


def norm(values, gain_row):
    average = jnp.mean(values, axis=-1, keepdims=True)
    centred = values - average
    variance = jnp.mean(centred * centred, axis=-1, keepdims=True)
    return (centred * lax.rsqrt(variance + norm_eps) * gain_row).astype(bf16)


def gelu(v):
    return 0.5 * v * (1.0 + jnp.tanh(math.sqrt(2.0 / math.pi) * (v + 0.044715 * (v * v * v))))


def exchange_blocks(arrays, width):
    arrays = list(arrays)
    lane = lax.broadcasted_iota(jnp.int32, arrays[0].shape, 1) // width
    step = 1
    while step < len(arrays):
        low = (lane // step) % 2 == 0
        for i in range(len(arrays)):
            if i & step == 0:
                a, b = arrays[i], arrays[i | step]
                arrays[i] = jnp.where(low, a, pltpu.roll(b, step * width, axis=1))
                arrays[i | step] = jnp.where(low, pltpu.roll(a, 128 - step * width, axis=1), b)
        step *= 2
    return arrays


def attention(queries, keys, values, left):
    outs = []
    for pair in range(HEADS // 2):
        lanes = slice(128 * pair, 128 * pair + 128)
        q, k, v = queries[:, lanes], keys[:, lanes], values[:, lanes]
        halves = []
        for which in range(2):
            q_one = jnp.where(left if which == 0 else ~left, q, jnp.zeros_like(q))
            scores = dot(q_one, k, NT)
            top = jnp.max(scores, axis=-1, keepdims=True)
            raised = jnp.exp(scores - top)
            total = jnp.sum(raised, axis=-1, keepdims=True)
            halves.append(dot(raised.astype(bf16), v) / total)
        outs.append(jnp.where(left, halves[0], halves[1]).astype(bf16))
    return jnp.concatenate(outs, axis=1)


def tail(hidden, attended, w_out, w_up, w_down, gain1, gain2):
    hidden = hidden + dot(attended, w_out[...])
    inner = gelu(dot(norm(hidden, gain1), w_up[...])).astype(bf16)
    hidden = hidden + dot(inner, w_down[...])
    return norm(hidden, gain2)


PARTS = 4
CHUNK = HALF // PARTS


def step_kernel(*refs):
    (
        consts, gains, noisy, noise, measured, cap,
        h_patch, h_qkv, h_out, h_up, h_down, h_unpatch,
        h_coarse, h_twist, h_fine, h_fine_t, h_order, h_swap, h_cast, h_deal, h_spill,
        previous, estimate,
        patch0, qkv0, out0, up0, down0, unpatch0,
        patch1, qkv1, out1, up1, down1, unpatch1,
        coarse, twist, fine, fine_t, order, swap, cast, deal, spill,
        strips, wide, cut, high_src, low_src, own_dst, oth_dst, low_dst, relay_src, relay_dst,
        tok, hidden, queries, pairs, guess, guess16, guess_dst,
        summed, turned, spread, line_src, line_dst,
        cells, fix_src, fix_dst, turned2, spread2, back_src, back_dst, blended,
        col_src, col_dst, final_src, final_dst,
        load_sem, send_sem, recv_sem, pair_send, pair_recv, ready,
    ) = refs
    gz, gy = lax.axis_index("gz"), lax.axis_index("gy")
    col, plane = gz // 2, lax.rem(gz, 2)
    mine = col * GY + gy
    me = gz * NY + lax.rem(gy, NY)
    keeps = plane == gy // NY
    partner = {"gz": 2 * col + 1 - plane}
    feat = consts[0:1, :]
    root_noise, inv_signal = consts[1:2, 0:1], consts[1:2, 1:2]

    plan = [
        (h_cast, cast), (h_swap, swap), (h_order, order), (h_patch.at[0], patch0),
        (h_qkv.at[0], qkv0), (h_out.at[0], out0), (h_up.at[0], up0), (h_down.at[0], down0),
        (h_unpatch.at[0], unpatch0), (h_coarse, coarse), (h_twist, twist),
        (h_fine.at[plane], fine), (h_fine_t.at[plane], fine_t),
        (h_patch.at[1], patch1), (h_qkv.at[1], qkv1), (h_out.at[1], out1), (h_up.at[1], up1),
        (h_down.at[1], down1), (h_unpatch.at[1], unpatch1), (h_deal, deal),
        (h_spill, spill),
    ]
    loads = [
        pltpu.make_async_copy(src, dst, load_sem.at[i]) for i, (src, dst) in enumerate(plan)
    ]
    for load in loads:
        load.start()

    barrier = pltpu.get_barrier_semaphore()
    for core in range(2):
        for k in range(1 - core, GY):
            where = {"gz": 2 * col + lax.rem(plane + core, 2), "gy": lax.rem(gy + k, GY)}
            pl.semaphore_signal(barrier, inc=1, device_id=where, device_id_type=MESH_ID)
        for k in range(1, GZ // 2):
            where = {"gz": 2 * lax.rem(col + k, GZ // 2) + core}
            pl.semaphore_signal(barrier, inc=1, device_id=where, device_id_type=MESH_ID)

    def remote(src, dst, send, recv, where):
        return pltpu.make_async_remote_copy(
            src_ref=src, dst_ref=dst, send_sem=send, recv_sem=recv,
            device_id=where, device_id_type=MESH_ID,
        )

    def send(src, dst, which, to_gz, to_gy):
        here = jnp.logical_and(to_gz == gz, to_gy == gy)

        @pl.when(here)
        def _():
            pltpu.make_async_copy(src, dst, recv_sem.at[which]).start()

        @pl.when(jnp.logical_not(here))
        def _():
            where = {"gz": to_gz, "gy": to_gy}
            remote(src, dst, send_sem.at[which], recv_sem.at[which], where).start()

    for g in range(4):
        strips[g] = noisy[:, 128 * g : 128 * g + 128]
        for part in range(2):
            rows = [strips[g, pl.ds(8 * part + i, 16, stride=16), :] for i in range(8)]
            for i, block in enumerate(exchange_blocks(rows, 16)):
                high = block.astype(bf16)
                at = slice((8 * g + i) * 16, (8 * g + i) * 16 + 16)
                cut[at, 128 * part : 128 * part + 128] = high
                cut[at, 256 + 128 * part : 384 + 128 * part] = (
                    block - high.astype(f32)
                ).astype(bf16)
    loads[0].wait()
    sorted_rows = dot(cast[...], cut[...]).astype(bf16).reshape(GY, 64, 512)
    high_src[...] = sorted_rows[:, :, :256]
    low_src[...] = sorted_rows[:, :, 256:]

    pl.semaphore_wait(barrier, 2 * GY - 1 + GZ - 2)

    def send_patches(src, dst, which):
        for k in range(NY):
            slot = lax.rem(gy + k, NY)
            for half in range(2):
                send(
                    src.at[half * NY + slot], dst.at[gy], which, 2 * col + half,
                    plane * NY + slot,
                )

    send_patches(high_src, own_dst, 0)
    peers = []
    for k in range(1, GY):
        peer = lax.rem(gy + k, GY)
        where = {"gy": peer}
        peers.append((peer, where))
        pl.semaphore_signal(ready, inc=1, device_id=where, device_id_type=MESH_ID)

    for s in range(2):
        for g in range(4):
            part = noisy[128 * s : 128 * s + 128, 128 * g : 128 * g + 128].T
            relay_src[4 * g : 4 * g + 4, :, 128 * s : 128 * s + 128] = part.reshape(4, 32, 128)

    relay_dst[gz] = relay_src[gz]

    for a in range(12):
        wide[a, :, 0:64] = measured[a] if a < 8 else cap[a - 8].astype(f32)
        quarter = [wide[a, pl.ds(q, 8, stride=4), :] for q in range(4)]
        for r in range(2):
            cells[a, 8 * r : 8 * r + 8, :] = jnp.concatenate(
                [v[:, 32 * r : 32 * r + 32] for v in quarter], axis=1
            )

    for load in loads[1:9]:
        load.wait()
    unpatch0[...] = dot(unpatch0[...], swap[...]).astype(bf16)

    def gather(dst, src, s, r, count):
        part = pl.ds(0, count)
        del src
        pltpu.make_async_copy(dst.at[part], dst.at[part], recv_sem.at[r]).wait()

    gather(own_dst, None, 0, 0, GY)
    swap_own = remote(own_dst, oth_dst, send_sem.at[1], recv_sem.at[1], partner)
    swap_own.start()
    send_patches(low_src, low_dst, 6)

    @pl.loop(1, GZ)
    def _(k):
        peer = lax.rem(gz + k, GZ)
        remote(
            relay_src.at[peer], relay_dst.at[gz], send_sem.at[2], recv_sem.at[2], {"gz": peer}
        ).start()

    tok[...] = dot(order[...], own_dst[...].reshape(HALF, 256)).astype(bf16)

    def gain(m, r):
        return gains[r, m : m + 1, :]

    first = dot(tok[...], patch0[...]) + feat
    hidden[...] = first
    normed = norm(first, gain(0, 0))
    queries[...] = (dot(normed, qkv0[:, :D]).astype(bf16) * 0.125).astype(bf16)
    pairs[0:HALF, :] = dot(normed, qkv0[:, D:]).astype(bf16)
    swap_own.wait()
    normed = norm(dot(oth_dst[...].reshape(HALF, 256), patch0[...]) + feat, gain(0, 0))
    pairs[HALF:, :] = dot(normed, qkv0[:, D:]).astype(bf16)

    left = lax.broadcasted_iota(jnp.int32, (HALF, 128), 1) < 64
    attended = attention(queries[...], pairs[:, :D], pairs[:, D:], left)
    queries[...] = tail(hidden[...], attended, out0, up0, down0, gain(0, 1), gain(0, 2))
    gather(low_dst, None, 6, 6, GY)
    low = dot(order[...], low_dst[...].reshape(HALF, 256)).astype(bf16)
    summed[:, 0:HALF] = dot(swap[...], tok[...], NT) + dot(swap[...], low, NT)
    for i in range(PARTS):
        at = slice(i * CHUNK, i * CHUNK + CHUNK)
        net = dot(unpatch0[...], queries[at, :], (((0,), (1,)), ((), ())))
        first = (summed[:, at] - root_noise * net) * inv_signal
        guess[:, at] = first
        guess16[i] = first.astype(bf16)
        remote(
            guess16.at[i], guess_dst.at[i], pair_send.at[i], pair_recv.at[i], partner
        ).start()

    for load in loads[9:13]:
        load.wait()
    half_rows = pl.ds(pl.multiple_of(plane * HALF, HALF), HALF)
    side_rows = pl.ds(pl.multiple_of((1 - plane) * HALF, HALF), HALF)
    held = jnp.concatenate([guess16[i] for i in range(PARTS)], axis=1)
    for c in range(4):
        at = slice(512 * c, 512 * c + 512)
        summed[:, at] = dot(held, coarse[half_rows, at])
    for i in range(PARTS):
        remote(
            guess16.at[i], guess_dst.at[i], pair_send.at[i], pair_recv.at[i], partner
        ).wait()
    theirs = jnp.concatenate([guess_dst[i] for i in range(PARTS)], axis=1)
    for c in range(4):
        at = slice(256 * c, 256 * c + 256)
        im = slice(1024 + 256 * c, 1280 + 256 * c)
        real = summed[:, at] + dot(theirs, coarse[side_rows, at])
        imag = summed[:, im] + dot(theirs, coarse[side_rows, im])
        t_re, t_im = twist[0, :, at], twist[1, :, at]
        turned[0:256, at] = (real * t_re - imag * t_im).astype(bf16)
        turned[256:512, at] = (real * t_im + imag * t_re).astype(bf16)

    pl.semaphore_wait(ready, GY - 1)

    @pl.loop(0, 4)
    def _(i):
        block = lax.rem(i + gz // 4, 4)
        res = dot(fine[pl.ds(pl.multiple_of(block * 64, 64), 64), :], turned[...])
        for c in range(8):
            spread[pl.ds(c, 64, stride=8), :] = res[:, 128 * c : 128 * c + 128]
        line_src[pl.ds(block * 16, 16)] = spread[...].astype(bf16).reshape(16, 2, 16, 128)

        @pl.loop(0, 16)
        def _(j):
            peer = block * 16 + j

            send(
                line_src.at[peer], line_dst.at[mine], 3, peer // NY, plane * NY + lax.rem(peer, NY)
            )

    angle = cells[8:12] * (2.0 * math.pi / NZ)
    w_re, w_im = jnp.cos(angle), -jnp.sin(angle)
    turns = lax.rem(cells[8:12].astype(jnp.int32) * mine, NZ).astype(f32) * (2.0 * math.pi / NZ)
    first_re, first_im = jnp.cos(turns), jnp.sin(turns)
    gather(line_dst, None, 3, 3, GROUP)

    def pick(i, state):
        p_re, p_im = state
        z = NZ - 1 - i
        x_re, x_im = line_dst[z, 0].astype(f32), line_dst[z, 1].astype(f32)
        return (
            p_re * w_re - p_im * w_im + x_re[None],
            p_re * w_im + p_im * w_re + x_im[None],
        )

    zero = jnp.zeros_like(w_re)
    p_re, p_im = lax.fori_loop(0, NZ, pick, (zero, zero), unroll=8)
    scale = 1.0 / math.sqrt(NZ)
    want = cells[0:8].reshape(4, 2, 16, 128)
    r_re = (want[:, 0] - p_re * scale) * scale
    r_im = (want[:, 1] - p_im * scale) * scale
    state = (r_re * first_re - r_im * first_im, r_re * first_im + r_im * first_re)

    def put(ref, z, state):
        t_re, t_im = state
        ref[z, 0] = (t_re[0] + t_re[1] + t_re[2] + t_re[3]).astype(bf16)
        ref[z, 1] = (t_im[0] + t_im[1] + t_im[2] + t_im[3]).astype(bf16)
        return (t_re * w_re + t_im * w_im, t_im * w_re - t_re * w_im)

    def expand(k, state):
        z = lax.rem(mine + k, NZ)
        state = put(fix_src, z, state)
        send(fix_src.at[z], fix_dst.at[me], 4, 2 * (z // GY) + gy // NY, lax.rem(z, GY))
        return state

    lax.fori_loop(0, GROUP, expand, state)

    gather(fix_dst, None, 4, 4, GROUP)
    spread2[...] = fix_dst[...].reshape(GROUP * 32, 128).astype(f32)
    for c in range(4):
        at = slice(c * 256, c * 256 + 256)
        block = jnp.concatenate(
            [spread2[pl.ds(2 * c + k, 256, stride=8), :].astype(bf16) for k in range(2)], axis=1
        )
        res = dot(fine_t[...], block)
        real, imag = res[:256], res[256:]
        t_re, t_im = twist[0, :, at], twist[1, :, at]
        turned2[:, at] = (real * t_re + imag * t_im).astype(bf16)
        turned2[:, 1024 + c * 256 : 1280 + c * 256] = (imag * t_re - real * t_im).astype(bf16)
    for c in range(2):
        rows = pl.ds(pl.multiple_of((1 - plane) * HALF + c * 256, 256), 256)
        back_src[c] = dot(turned2[...], coarse[rows, :], NT).astype(bf16)
        remote(
            back_src.at[c], back_dst.at[c], pair_send.at[PARTS + c], pair_recv.at[PARTS + c],
            partner,
        ).start()
    for c in range(2):
        rows = pl.ds(pl.multiple_of(plane * HALF + c * 256, 256), 256)
        at = slice(c * 256, c * 256 + 256)
        blended[:, at] = guess[:, at] + dot(turned2[...], coarse[rows, :], NT)
    for c in range(2):
        at = slice(c * 256, c * 256 + 256)
        remote(
            back_src.at[c], back_dst.at[c], pair_send.at[PARTS + c], pair_recv.at[PARTS + c],
            partner,
        ).wait()
        blended[:, at] = blended[:, at] + back_dst[c].astype(f32)

    for q in range(4):
        for g in range(4):
            rows = [
                blended[q * 64 + r * 16 : q * 64 + r * 16 + 16, 128 * g : 128 * g + 128]
                for r in range(4)
            ]
            for i, block in enumerate(exchange_blocks(rows, 32)):
                col_src[(4 * g + i) * 4 + q] = block.astype(bf16)

    @pl.loop(0, GROUP)
    def _(k):
        peer = lax.rem(me + k, GROUP)
        send(col_src.at[peer], col_dst.at[mine], 5, peer // NY, plane * NY + lax.rem(peer, NY))

    gather(relay_dst, None, 2, 2, GZ - 1)
    c_est, c_old, c_new = consts[1:2, 2:3], consts[1:2, 3:4], consts[1:2, 4:5]

    @pl.loop(0, GZ)
    def _(i):
        for z in range(4):
            previous[4 * i + z] = (
                c_old * relay_dst[i, :, 64 * z : 64 * z + 64] + c_new * noise[4 * i + z]
            )

    for load in loads[13:]:
        load.wait()
    patch1[...] = dot(swap[...], patch1[...]).astype(bf16)
    unpatch1[...] = dot(unpatch1[...], swap[...]).astype(bf16)
    gather(col_dst, None, 5, 5, GROUP)
    for zb in range(4):
        pix = col_dst[zb * 16 : zb * 16 + 16].reshape(256, 128)
        first = dot(pix, patch1[...], TN) + feat
        for x in range(4):
            hidden[x * 128 + zb * 32 : x * 128 + zb * 32 + 32, :] = first[32 * x : 32 * x + 32, :]
    normed = norm(hidden[...], gain(1, 0))
    queries[...] = (dot(normed, qkv1[:, :D]).astype(bf16) * 0.125).astype(bf16)
    pairs[0:HALF, :] = dot(normed, qkv1[:, D:]).astype(bf16)
    left1 = lax.broadcasted_iota(jnp.int32, (128, 128), 1) < 64
    for p in range(2):
        half = slice(256 * p, 256 * p + 256)
        attended = []
        for x in range(2):
            at = slice(256 * p + 128 * x, 256 * p + 128 * x + 128)
            attended.append(attention(queries[at, :], pairs[at, :D], pairs[at, D:], left1))
        attended = jnp.concatenate(attended, axis=0)
        normed = tail(hidden[half, :], attended, out1, up1, down1, gain(1, 1), gain(1, 2))
        moved = dot(deal[...], normed).astype(bf16)
        value = root_noise * dot(moved, unpatch1[...])
        for zb in range(4):
            pix = col_dst[zb * 16 : zb * 16 + 16].reshape(256, 128)
            value = value + dot(spill[p, :, 128 * zb : 128 * zb + 128], pix, NT)
        for h in range(2):
            final_src[p, :, h] = value[:, 128 * h : 128 * h + 128].reshape(GY, 32, 128)
        here = pl.ds(pl.multiple_of(gy * 64 + p * 32, 32), 32)
        for peer, where in peers:
            remote(
                final_src.at[p, peer], final_dst.at[:, here, :], send_sem.at[7], recv_sem.at[7],
                where,
            ).start()
        final_dst[:, here, :] = final_src[p, gy]

    def drain(src, which, count):
        part = pl.ds(0, count)
        pltpu.make_async_copy(src.at[part], src.at[part], send_sem.at[which]).wait()

    def drain_kept(kept):
        drain(high_src, 0, GY - kept)
        drain(low_src, 6, GY - kept)
        drain(line_src, 3, GROUP - kept)
        drain(fix_src, 4, GROUP - kept)
        drain(col_src, 5, GROUP - kept)

    @pl.when(keeps)
    def _():
        drain_kept(1)

    @pl.when(jnp.logical_not(keeps))
    def _():
        drain_kept(0)

    drain(relay_src, 2, GZ - 1)
    done = final_dst.at[:, pl.ds(0, (GY - 1) * 64), :]
    pltpu.make_async_copy(done, done, send_sem.at[7]).wait()
    pltpu.make_async_copy(done, done, recv_sem.at[7]).wait()

    for g in range(4):
        at = slice(8 * g, 8 * g + 8)
        for zb in range(4):
            for h in range(2):
                blocks = [
                    final_dst[h, pl.ds(128 * g + zb * 4 + yb, 8, stride=16), :] for yb in range(4)
                ]
                for i, block in enumerate(exchange_blocks(blocks, 16)):
                    for part in range(2):
                        z = zb * 16 + h * 8 + part * 4 + i
                        value = block[:, 64 * part : 64 * part + 64]
                        estimate[z, at, :] = value
                        previous[z, at, :] = previous[z, at, :] + c_est * value


def local(
    noisy, noise, timestep, measured, cap_index, w_patch, w_qkv, w_out, w_up, w_down, w_unpatch,
    norm_gain,
):
    moment = timestep[0].astype(f32)
    signal_now = cumulative_alpha(moment)
    signal_prev = cumulative_alpha(moment - STRIDE)
    root_signal = jnp.sqrt(signal_now)
    root_noise = jnp.sqrt(1.0 - signal_now)
    toward = jnp.sqrt(
        (1.0 - signal_prev) * signal_now * (1.0 / signal_prev - 1.0) / (1.0 - signal_now)
    )
    spread = jnp.sqrt((1.0 - signal_prev) / (1.0 - signal_now) * (1.0 - signal_now / signal_prev))
    coefs = (
        root_noise, 1.0 / root_signal, jnp.sqrt(signal_prev) - toward * root_signal / root_noise,
        toward / root_noise, spread,
    )
    place = lax.broadcasted_iota(jnp.int32, (1, D), 1)
    row = jnp.zeros((1, D), f32)
    for i, value in enumerate(coefs):
        row = jnp.where(place == i, value, row)
    consts = jnp.concatenate([time_features(moment)[None], row], axis=0)
    vmem = pl.BlockSpec(memory_space=pltpu.VMEM)
    anywhere = pl.BlockSpec(memory_space=pl.ANY)
    V = pltpu.VMEM
    weights = lambda: [
        V((PIX, D), bf16), V((D, 3 * D), bf16), V((D, D), bf16), V((D, FF), bf16),
        V((FF, D), bf16), V((D, PIX), bf16),
    ]
    shape = jax.ShapeDtypeStruct((NZ, 32, 64), f32)
    previous, estimate = pl.pallas_call(
        step_kernel,
        out_shape=(shape, shape),
        in_specs=[vmem] * 6 + [anywhere] * 15,
        out_specs=(vmem, vmem),
        scratch_shapes=weights() + weights() + [
            V((1024, 2048), bf16), V((2, 256, 1024), f32), V((256, 512), bf16),
            V((512, 256), bf16), V((512, 512), bf16), V((256, 256), bf16),
            V((512, 512), bf16), V((256, 256), bf16), V((2, 256, 512), bf16),
            V((4, 256, 128), f32), V((12, 32, 128), f32), V((512, 512), bf16),
            V((GY, 64, 256), bf16), V((GY, 64, 256), bf16), V((GY, 64, 256), bf16),
            V((GY, 64, 256), bf16), V((GY, 64, 256), bf16),
            V((GZ, 32, 256), f32), V((GZ, 32, 256), f32),
            V((HALF, PIX), bf16), V((HALF, D), f32), V((HALF, D), bf16),
            V((2 * HALF, 2 * D), bf16), V((PIX, HALF), f32), V((PARTS, PIX, CHUNK), bf16),
            V((PARTS, PIX, CHUNK), bf16),
            V((PIX, 2048), f32), V((512, 1024), bf16), V((512, 128), f32),
            V((GROUP, 2, 16, 128), bf16), V((GROUP, 2, 16, 128), bf16),
            V((12, 16, 128), f32), V((GROUP, 2, 16, 128), bf16), V((GROUP, 2, 16, 128), bf16),
            V((PIX, 2048), bf16), V((GROUP * 32, 128), f32), V((2, PIX, 256), bf16),
            V((2, PIX, 256), bf16), V((PIX, HALF), f32),
            V((GROUP, 16, 128), bf16), V((GROUP, 16, 128), bf16),
            V((2, GY, 2, 32, 128), f32), V((2, 512, 128), f32),
            pltpu.SemaphoreType.DMA((21,)), pltpu.SemaphoreType.DMA((8,)),
            pltpu.SemaphoreType.DMA((8,)), pltpu.SemaphoreType.DMA((PARTS + 2,)),
            pltpu.SemaphoreType.DMA((PARTS + 2,)), pltpu.SemaphoreType.REGULAR,
        ],
        compiler_params=pltpu.CompilerParams(
            collective_id=0, has_side_effects=True, vmem_limit_bytes=58 * MIB
        ),
    )(
        consts, norm_gain.transpose(1, 0, 2), noisy.reshape(256, LAT), noise.transpose(0, 2, 1),
        measured.reshape(8, 32, 64), cap_index,
        w_patch, w_qkv, w_out, w_up, w_down, w_unpatch, *(jnp.asarray(t) for t in tables()),
    )
    return (previous.transpose(0, 2, 1), estimate.transpose(0, 2, 1))


def solution(mesh):
    placed = (
        P("gz", "gy", None),
        P(None, "gy", "gz"),
        P(),
        P(None, None, "gz", "gy"),
        P(None, "gz", "gy"),
    ) + (P(),) * 7
    return jax.shard_map(
        local,
        mesh=mesh,
        in_specs=placed,
        out_specs=(P(None, "gy", "gz"), P(None, "gy", "gz")),
        check_vma=False,
    )
```

```python
import math

import jax
import jax.numpy as jnp
import numpy as np
from jax import lax
from jax.experimental import pallas as pl
from jax.experimental.pallas import tpu as pltpu
from jax.sharding import PartitionSpec as P

PATCH = 16
D = 384
HEADS = 6
FF = 1536
TRAIN_STEPS = 1000
STRIDE = 100
NZ = 64
LAT = 512
GZ = 16
GY = 8
NY = 4
GROUP = GZ * NY
SIDE = LAT // PATCH
HALF = SIDE * SIDE // 2
PIX = PATCH * PATCH
norm_eps = 1e-05
MIB = 1024 * 1024
f32 = jnp.float32
bf16 = jnp.bfloat16
MESH_ID = pl.DeviceIdType.MESH
NT = (((1,), (1,)), ((), ()))
TN = (((0,), (0,)), ((), ()))


def tables():
    parity, half_x, block_y = np.meshgrid(np.arange(2), np.arange(16), np.arange(32), indexing="ij")
    block_x = (2 * half_x + parity).reshape(-1)
    block_y = block_y.reshape(-1)
    by, bx = np.meshgrid(np.arange(32), np.arange(32), indexing="ij")
    by, bx = by.reshape(-1), bx.reshape(-1)
    turn = 2 * np.pi * ((block_y[:, None] * by[None] + block_x[:, None] * bx[None]) % 32) / 32
    coarse = np.concatenate([np.cos(turn), -np.sin(turn)], axis=1)
    xi, yi = np.meshgrid(np.arange(16), np.arange(16), indexing="ij")
    xi, yi = xi.reshape(-1), yi.reshape(-1)
    turn = 2 * np.pi * ((yi[:, None] * by[None] + xi[:, None] * bx[None]) % 512) / 512
    twist = np.stack([np.cos(turn), -np.sin(turn)]) / 32.0
    fine = np.zeros((2, 16, 4, 2, 2, 2, 256))
    for half in range(2):
        for quarter in range(4):
            for rest in range(2):
                ax = 8 * half + 2 * quarter + rest
                turn = 2 * np.pi * ((np.arange(16)[:, None] * yi[None] + ax * xi[None]) % 16) / 16
                fine[half, :, quarter, 0, rest, 0] = np.cos(turn)
                fine[half, :, quarter, 0, rest, 1] = np.sin(turn)
                fine[half, :, quarter, 1, rest, 0] = -np.sin(turn)
                fine[half, :, quarter, 1, rest, 1] = np.cos(turn)
    fine = fine.reshape(2, 256, 512) / 16.0
    to_bf = lambda a: a.astype(jnp.bfloat16)
    order = np.zeros((512, 512), np.float32)
    for gy in range(8):
        for hx in range(16):
            for yb in range(4):
                order[hx * 32 + gy * 4 + yb, gy * 64 + hx * 4 + yb] = 1.0
    swap = np.zeros((256, 256), np.float32)
    for y in range(16):
        for x in range(16):
            swap[x * 16 + y, y * 16 + x] = 1.0
    cast = np.zeros((512, 512), np.float32)
    for xb in range(32):
        for s in range(4):
            for yb in range(4):
                cast[(xb % 2) * 256 + s * 64 + (xb // 2) * 4 + yb, xb * 16 + s * 4 + yb] = 1.0
    deal = np.zeros((256, 256), np.float32)
    spill = np.zeros((2, 256, 512), np.float32)
    for x in range(4):
        for zb in range(4):
            for yb in range(32):
                row = (yb // 4) * 32 + (x % 2) * 16 + zb * 4 + yb % 4
                deal[row, (x % 2) * 128 + zb * 32 + yb] = 1.0
                spill[x // 2, row, zb * 128 + x * 32 + yb] = 1.0
    return (
        to_bf(coarse),
        twist.astype(np.float32),
        to_bf(fine),
        to_bf(np.ascontiguousarray(fine.transpose(0, 2, 1))),
        to_bf(order),
        to_bf(swap),
        to_bf(cast),
        to_bf(deal),
        to_bf(spill),
    )


def cumulative_alpha(moment):
    phase_angle = (moment / TRAIN_STEPS + 0.008) / 1.008 * (math.pi / 2.0)
    return jnp.cos(phase_angle) ** 2


def time_features(moment):
    half_width = D // 2
    frequency = jnp.exp(
        -math.log(10000.0) * jnp.arange(half_width).astype(jnp.float32) / half_width
    )
    angles = moment * frequency
    return jnp.concatenate([jnp.sin(angles), jnp.cos(angles)])


def dot(a, b, dims=None):
    if dims is None:
        return jnp.dot(a, b, preferred_element_type=f32)
    return lax.dot_general(a, b, dims, preferred_element_type=f32)


def norm(values, gain_row):
    average = jnp.mean(values, axis=-1, keepdims=True)
    centred = values - average
    variance = jnp.mean(centred * centred, axis=-1, keepdims=True)
    return (centred * lax.rsqrt(variance + norm_eps) * gain_row).astype(bf16)


def gelu(v):
    return 0.5 * v * (1.0 + jnp.tanh(math.sqrt(2.0 / math.pi) * (v + 0.044715 * (v * v * v))))


def exchange_blocks(arrays, width):
    arrays = list(arrays)
    lane = lax.broadcasted_iota(jnp.int32, arrays[0].shape, 1) // width
    step = 1
    while step < len(arrays):
        low = (lane // step) % 2 == 0
        for i in range(len(arrays)):
            if i & step == 0:
                a, b = arrays[i], arrays[i | step]
                arrays[i] = jnp.where(low, a, pltpu.roll(b, step * width, axis=1))
                arrays[i | step] = jnp.where(low, pltpu.roll(a, 128 - step * width, axis=1), b)
        step *= 2
    return arrays


def attention(queries, keys, values, left):
    outs = []
    for pair in range(HEADS // 2):
        lanes = slice(128 * pair, 128 * pair + 128)
        q, k, v = queries[:, lanes], keys[:, lanes], values[:, lanes]
        halves = []
        for which in range(2):
            q_one = jnp.where(left if which == 0 else ~left, q, jnp.zeros_like(q))
            scores = dot(q_one, k, NT)
            top = jnp.max(scores, axis=-1, keepdims=True)
            raised = jnp.exp(scores - top)
            total = jnp.sum(raised, axis=-1, keepdims=True)
            halves.append(dot(raised.astype(bf16), v) / total)
        outs.append(jnp.where(left, halves[0], halves[1]).astype(bf16))
    return jnp.concatenate(outs, axis=1)


def tail(hidden, attended, w_out, w_up, w_down, gain1, gain2):
    hidden = hidden + dot(attended, w_out[...])
    inner = gelu(dot(norm(hidden, gain1), w_up[...])).astype(bf16)
    hidden = hidden + dot(inner, w_down[...])
    return norm(hidden, gain2)


PARTS = 4
CHUNK = HALF // PARTS


def step_kernel(*refs):
    (
        consts, gains, noisy, measured, cap, h_noise,
        h_patch, h_qkv, h_out, h_up, h_down, h_unpatch,
        h_coarse, h_twist, h_fine, h_fine_t, h_order, h_swap, h_cast, h_deal, h_spill,
        base, scaled,
        patch0, qkv0, out0, up0, down0, unpatch0,
        patch1, qkv1, out1, up1, down1, unpatch1,
        coarse, twist, fine, fine_t, order, swap, cast, deal, spill,
        noise, strips, wide, cut, high_src, low_src, own_dst, oth_dst, low_dst, relay_src, relay_dst,
        tok, hidden, queries, pairs, guess, guess16, guess_dst,
        summed, turned, spread, line_src, line_dst,
        cells, fix_src, fix_dst, turned2, spread2, back_src, back_dst, blended,
        col_src, col_dst, final_src, final_dst,
        load_sem, send_sem, recv_sem, pair_send, pair_recv, ready,
    ) = refs
    gz, gy = lax.axis_index("gz"), lax.axis_index("gy")
    col, plane = gz // 2, lax.rem(gz, 2)
    mine = col * GY + gy
    me = gz * NY + lax.rem(gy, NY)
    keeps = plane == gy // NY
    partner = {"gz": 2 * col + 1 - plane}
    feat = consts[0:1, :]
    root_noise, inv_signal = consts[1:2, 0:1], consts[1:2, 1:2]

    plan = [
        (h_cast, cast), (h_swap, swap), (h_order, order), (h_patch.at[0], patch0),
        (h_qkv.at[0], qkv0), (h_out.at[0], out0), (h_up.at[0], up0), (h_down.at[0], down0),
        (h_unpatch.at[0], unpatch0), (h_coarse, coarse), (h_twist, twist),
        (h_fine.at[plane], fine), (h_fine_t.at[plane], fine_t),
        (h_patch.at[1], patch1), (h_qkv.at[1], qkv1), (h_out.at[1], out1), (h_up.at[1], up1),
        (h_down.at[1], down1), (h_unpatch.at[1], unpatch1), (h_deal, deal),
        (h_spill, spill), (h_noise, noise),
    ]
    loads = [
        pltpu.make_async_copy(src, dst, load_sem.at[i]) for i, (src, dst) in enumerate(plan)
    ]
    for load in loads:
        load.start()

    barrier = pltpu.get_barrier_semaphore()
    for core in range(2):
        for k in range(1 - core, GY):
            where = {"gz": 2 * col + lax.rem(plane + core, 2), "gy": lax.rem(gy + k, GY)}
            pl.semaphore_signal(barrier, inc=1, device_id=where, device_id_type=MESH_ID)
        for k in range(1, GZ // 2):
            where = {"gz": 2 * lax.rem(col + k, GZ // 2) + core}
            pl.semaphore_signal(barrier, inc=1, device_id=where, device_id_type=MESH_ID)

    def remote(src, dst, send, recv, where):
        return pltpu.make_async_remote_copy(
            src_ref=src, dst_ref=dst, send_sem=send, recv_sem=recv,
            device_id=where, device_id_type=MESH_ID,
        )

    def send(src, dst, which, to_gz, to_gy):
        here = jnp.logical_and(to_gz == gz, to_gy == gy)

        @pl.when(here)
        def _():
            pltpu.make_async_copy(src, dst, recv_sem.at[which]).start()

        @pl.when(jnp.logical_not(here))
        def _():
            where = {"gz": to_gz, "gy": to_gy}
            remote(src, dst, send_sem.at[which], recv_sem.at[which], where).start()

    for g in range(4):
        strips[g] = noisy[:, 128 * g : 128 * g + 128]
        for part in range(2):
            rows = [strips[g, pl.ds(8 * part + i, 16, stride=16), :] for i in range(8)]
            for i, block in enumerate(exchange_blocks(rows, 16)):
                high = block.astype(bf16)
                at = slice((8 * g + i) * 16, (8 * g + i) * 16 + 16)
                cut[at, 128 * part : 128 * part + 128] = high
                cut[at, 256 + 128 * part : 384 + 128 * part] = (
                    block - high.astype(f32)
                ).astype(bf16)
    loads[0].wait()
    sorted_rows = dot(cast[...], cut[...]).astype(bf16).reshape(GY, 64, 512)
    high_src[...] = sorted_rows[:, :, :256]
    low_src[...] = sorted_rows[:, :, 256:]

    pl.semaphore_wait(barrier, 2 * GY - 1 + GZ - 2)

    def send_patches(src, dst, which):
        for k in range(NY):
            slot = lax.rem(gy + k, NY)
            for half in range(2):
                send(
                    src.at[half * NY + slot], dst.at[gy], which, 2 * col + half,
                    plane * NY + slot,
                )

    send_patches(high_src, own_dst, 0)
    peers = []
    for k in range(1, GY):
        peer = lax.rem(gy + k, GY)
        where = {"gy": peer}
        peers.append((peer, where))
        pl.semaphore_signal(ready, inc=1, device_id=where, device_id_type=MESH_ID)

    for s in range(2):
        for g in range(4):
            part = noisy[128 * s : 128 * s + 128, 128 * g : 128 * g + 128].T
            relay_src[4 * g : 4 * g + 4, :, 128 * s : 128 * s + 128] = part.reshape(4, 32, 128)

    relay_dst[gz] = relay_src[gz]

    for a in range(12):
        wide[a, :, 0:64] = measured[a] if a < 8 else cap[a - 8].astype(f32)
        quarter = [wide[a, pl.ds(q, 8, stride=4), :] for q in range(4)]
        for r in range(2):
            cells[a, 8 * r : 8 * r + 8, :] = jnp.concatenate(
                [v[:, 32 * r : 32 * r + 32] for v in quarter], axis=1
            )

    for load in loads[1:9]:
        load.wait()
    unpatch0[...] = dot(unpatch0[...], swap[...]).astype(bf16)

    def gather(dst, src, s, r, count):
        part = pl.ds(0, count)
        del src
        pltpu.make_async_copy(dst.at[part], dst.at[part], recv_sem.at[r]).wait()

    gather(own_dst, None, 0, 0, GY)
    swap_own = remote(own_dst, oth_dst, send_sem.at[1], recv_sem.at[1], partner)
    swap_own.start()
    send_patches(low_src, low_dst, 6)

    @pl.loop(1, GZ)
    def _(k):
        peer = lax.rem(gz + k, GZ)
        remote(
            relay_src.at[peer], relay_dst.at[gz], send_sem.at[2], recv_sem.at[2], {"gz": peer}
        ).start()

    tok[...] = dot(order[...], own_dst[...].reshape(HALF, 256)).astype(bf16)

    def gain(m, r):
        return gains[r, m : m + 1, :]

    first = dot(tok[...], patch0[...]) + feat
    hidden[...] = first
    normed = norm(first, gain(0, 0))
    queries[...] = (dot(normed, qkv0[:, :D]).astype(bf16) * 0.125).astype(bf16)
    pairs[0:HALF, :] = dot(normed, qkv0[:, D:]).astype(bf16)
    swap_own.wait()
    normed = norm(dot(oth_dst[...].reshape(HALF, 256), patch0[...]) + feat, gain(0, 0))
    pairs[HALF:, :] = dot(normed, qkv0[:, D:]).astype(bf16)

    left = lax.broadcasted_iota(jnp.int32, (HALF, 128), 1) < 64
    attended = attention(queries[...], pairs[:, :D], pairs[:, D:], left)
    queries[...] = tail(hidden[...], attended, out0, up0, down0, gain(0, 1), gain(0, 2))
    gather(low_dst, None, 6, 6, GY)
    low = dot(order[...], low_dst[...].reshape(HALF, 256)).astype(bf16)
    summed[:, 0:HALF] = dot(swap[...], tok[...], NT) + dot(swap[...], low, NT)
    for i in range(PARTS):
        at = slice(i * CHUNK, i * CHUNK + CHUNK)
        net = dot(unpatch0[...], queries[at, :], (((0,), (1,)), ((), ())))
        first = (summed[:, at] - root_noise * net) * inv_signal
        guess[:, at] = first
        guess16[i] = first.astype(bf16)
        remote(
            guess16.at[i], guess_dst.at[i], pair_send.at[i], pair_recv.at[i], partner
        ).start()

    for load in loads[9:13]:
        load.wait()
    half_rows = pl.ds(pl.multiple_of(plane * HALF, HALF), HALF)
    side_rows = pl.ds(pl.multiple_of((1 - plane) * HALF, HALF), HALF)
    held = jnp.concatenate([guess16[i] for i in range(PARTS)], axis=1)
    for c in range(4):
        at = slice(512 * c, 512 * c + 512)
        summed[:, at] = dot(held, coarse[half_rows, at])
    for i in range(PARTS):
        remote(
            guess16.at[i], guess_dst.at[i], pair_send.at[i], pair_recv.at[i], partner
        ).wait()
    theirs = jnp.concatenate([guess_dst[i] for i in range(PARTS)], axis=1)
    for c in range(4):
        at = slice(256 * c, 256 * c + 256)
        im = slice(1024 + 256 * c, 1280 + 256 * c)
        real = summed[:, at] + dot(theirs, coarse[side_rows, at])
        imag = summed[:, im] + dot(theirs, coarse[side_rows, im])
        t_re, t_im = twist[0, :, at], twist[1, :, at]
        turned[0:256, at] = (real * t_re - imag * t_im).astype(bf16)
        turned[256:512, at] = (real * t_im + imag * t_re).astype(bf16)

    pl.semaphore_wait(ready, GY - 1)

    @pl.loop(0, 4)
    def _(i):
        block = lax.rem(i + gz // 4, 4)
        res = dot(fine[pl.ds(pl.multiple_of(block * 64, 64), 64), :], turned[...])
        for c in range(8):
            spread[pl.ds(c, 64, stride=8), :] = res[:, 128 * c : 128 * c + 128]
        line_src[pl.ds(block * 16, 16)] = spread[...].astype(bf16).reshape(16, 2, 16, 128)

        @pl.loop(0, 16)
        def _(j):
            peer = block * 16 + j

            send(
                line_src.at[peer], line_dst.at[mine], 3, peer // NY, plane * NY + lax.rem(peer, NY)
            )

    angle = cells[8:12] * (2.0 * math.pi / NZ)
    w_re, w_im = jnp.cos(angle), -jnp.sin(angle)
    turns = lax.rem(cells[8:12].astype(jnp.int32) * mine, NZ).astype(f32) * (2.0 * math.pi / NZ)
    first_re, first_im = jnp.cos(turns), jnp.sin(turns)
    gather(line_dst, None, 3, 3, GROUP)

    def pick(i, state):
        p_re, p_im = state
        z = NZ - 1 - i
        x_re, x_im = line_dst[z, 0].astype(f32), line_dst[z, 1].astype(f32)
        return (
            p_re * w_re - p_im * w_im + x_re[None],
            p_re * w_im + p_im * w_re + x_im[None],
        )

    zero = jnp.zeros_like(w_re)
    p_re, p_im = lax.fori_loop(0, NZ, pick, (zero, zero), unroll=8)
    scale = 1.0 / math.sqrt(NZ)
    want = cells[0:8].reshape(4, 2, 16, 128)
    r_re = (want[:, 0] - p_re * scale) * scale
    r_im = (want[:, 1] - p_im * scale) * scale
    state = (r_re * first_re - r_im * first_im, r_re * first_im + r_im * first_re)

    def put(ref, z, state):
        t_re, t_im = state
        ref[z, 0] = (t_re[0] + t_re[1] + t_re[2] + t_re[3]).astype(bf16)
        ref[z, 1] = (t_im[0] + t_im[1] + t_im[2] + t_im[3]).astype(bf16)
        return (t_re * w_re + t_im * w_im, t_im * w_re - t_re * w_im)

    def expand(k, state):
        z = lax.rem(mine + k, NZ)
        state = put(fix_src, z, state)
        send(fix_src.at[z], fix_dst.at[me], 4, 2 * (z // GY) + gy // NY, lax.rem(z, GY))
        return state

    lax.fori_loop(0, GROUP, expand, state)

    gather(fix_dst, None, 4, 4, GROUP)
    spread2[...] = fix_dst[...].reshape(GROUP * 32, 128).astype(f32)
    for c in range(4):
        at = slice(c * 256, c * 256 + 256)
        block = jnp.concatenate(
            [spread2[pl.ds(2 * c + k, 256, stride=8), :].astype(bf16) for k in range(2)], axis=1
        )
        res = dot(fine_t[...], block)
        real, imag = res[:256], res[256:]
        t_re, t_im = twist[0, :, at], twist[1, :, at]
        turned2[:, at] = (real * t_re + imag * t_im).astype(bf16)
        turned2[:, 1024 + c * 256 : 1280 + c * 256] = (imag * t_re - real * t_im).astype(bf16)
    for c in range(2):
        rows = pl.ds(pl.multiple_of((1 - plane) * HALF + c * 256, 256), 256)
        back_src[c] = dot(turned2[...], coarse[rows, :], NT).astype(bf16)
        remote(
            back_src.at[c], back_dst.at[c], pair_send.at[PARTS + c], pair_recv.at[PARTS + c],
            partner,
        ).start()
    for c in range(2):
        rows = pl.ds(pl.multiple_of(plane * HALF + c * 256, 256), 256)
        at = slice(c * 256, c * 256 + 256)
        blended[:, at] = guess[:, at] + dot(turned2[...], coarse[rows, :], NT)
    for c in range(2):
        at = slice(c * 256, c * 256 + 256)
        remote(
            back_src.at[c], back_dst.at[c], pair_send.at[PARTS + c], pair_recv.at[PARTS + c],
            partner,
        ).wait()
        blended[:, at] = blended[:, at] + back_dst[c].astype(f32)

    for q in range(4):
        for g in range(4):
            rows = [
                blended[q * 64 + r * 16 : q * 64 + r * 16 + 16, 128 * g : 128 * g + 128]
                for r in range(4)
            ]
            for i, block in enumerate(exchange_blocks(rows, 32)):
                col_src[(4 * g + i) * 4 + q] = block.astype(bf16)

    @pl.loop(0, GROUP)
    def _(k):
        peer = lax.rem(me + k, GROUP)
        send(col_src.at[peer], col_dst.at[mine], 5, peer // NY, plane * NY + lax.rem(peer, NY))

    for load in loads[13:]:
        load.wait()
    gather(relay_dst, None, 2, 2, GZ - 1)
    c_old, c_new, inv_noise = consts[1:2, 3:4], consts[1:2, 4:5], consts[1:2, 5:6]

    @pl.loop(0, GZ)
    def _(i):
        for z in range(4):
            noise[4 * i + z] = (
                c_old * relay_dst[i, :, 64 * z : 64 * z + 64] + c_new * noise[4 * i + z]
            )

    store = pltpu.make_async_copy(noise, base, load_sem.at[len(plan)])
    store.start()

    patch1[...] = dot(swap[...], patch1[...]).astype(bf16)
    unpatch1[...] = dot(unpatch1[...], swap[...]).astype(bf16)
    gather(col_dst, None, 5, 5, GROUP)
    for zb in range(4):
        pix = col_dst[zb * 16 : zb * 16 + 16].reshape(256, 128)
        first = dot(pix, patch1[...], TN) + feat
        for x in range(4):
            hidden[x * 128 + zb * 32 : x * 128 + zb * 32 + 32, :] = first[32 * x : 32 * x + 32, :]
    normed = norm(hidden[...], gain(1, 0))
    queries[...] = (dot(normed, qkv1[:, :D]).astype(bf16) * 0.125).astype(bf16)
    pairs[0:HALF, :] = dot(normed, qkv1[:, D:]).astype(bf16)
    left1 = lax.broadcasted_iota(jnp.int32, (128, 128), 1) < 64
    for p in range(2):
        half = slice(256 * p, 256 * p + 256)
        attended = []
        for x in range(2):
            at = slice(256 * p + 128 * x, 256 * p + 128 * x + 128)
            attended.append(attention(queries[at, :], pairs[at, :D], pairs[at, D:], left1))
        attended = jnp.concatenate(attended, axis=0)
        normed = tail(hidden[half, :], attended, out1, up1, down1, gain(1, 1), gain(1, 2))
        moved = dot(deal[...], normed).astype(bf16)
        value = jnp.zeros((256, 256), f32)
        for zb in range(4):
            pix = col_dst[zb * 16 : zb * 16 + 16].reshape(256, 128)
            value = value + dot(spill[p, :, 128 * zb : 128 * zb + 128], pix, NT)
        value = value * inv_noise + dot(moved, unpatch1[...])
        for h in range(2):
            final_src[p, :, h] = value[:, 128 * h : 128 * h + 128].reshape(GY, 32, 128)
        here = pl.ds(pl.multiple_of(gy * 64 + p * 32, 32), 32)
        for peer, where in peers:
            remote(
                final_src.at[p, peer], final_dst.at[:, here, :], send_sem.at[7], recv_sem.at[7],
                where,
            ).start()
        final_dst[:, here, :] = final_src[p, gy]

    def drain(src, which, count):
        part = pl.ds(0, count)
        pltpu.make_async_copy(src.at[part], src.at[part], send_sem.at[which]).wait()

    def drain_kept(kept):
        drain(high_src, 0, GY - kept)
        drain(low_src, 6, GY - kept)
        drain(line_src, 3, GROUP - kept)
        drain(fix_src, 4, GROUP - kept)
        drain(col_src, 5, GROUP - kept)

    @pl.when(keeps)
    def _():
        drain_kept(1)

    @pl.when(jnp.logical_not(keeps))
    def _():
        drain_kept(0)

    drain(relay_src, 2, GZ - 1)
    done = final_dst.at[:, pl.ds(0, (GY - 1) * 64), :]
    pltpu.make_async_copy(done, done, send_sem.at[7]).wait()
    pltpu.make_async_copy(done, done, recv_sem.at[7]).wait()

    for g in range(4):
        at = slice(8 * g, 8 * g + 8)
        for zb in range(4):
            for h in range(2):
                blocks = [
                    final_dst[h, pl.ds(128 * g + zb * 4 + yb, 8, stride=16), :] for yb in range(4)
                ]
                for i, block in enumerate(exchange_blocks(blocks, 16)):
                    for part in range(2):
                        z = zb * 16 + h * 8 + part * 4 + i
                        value = block[:, 64 * part : 64 * part + 64]
                        scaled[z, at, :] = value
    store.wait()


def local(
    noisy, noise, timestep, measured, cap_index, w_patch, w_qkv, w_out, w_up, w_down, w_unpatch,
    norm_gain,
):
    moment = timestep[0].astype(f32)
    signal_now = cumulative_alpha(moment)
    signal_prev = cumulative_alpha(moment - STRIDE)
    root_signal = jnp.sqrt(signal_now)
    root_noise = jnp.sqrt(1.0 - signal_now)
    toward = jnp.sqrt(
        (1.0 - signal_prev) * signal_now * (1.0 / signal_prev - 1.0) / (1.0 - signal_now)
    )
    spread = jnp.sqrt((1.0 - signal_prev) / (1.0 - signal_now) * (1.0 - signal_now / signal_prev))
    coefs = (
        root_noise, 1.0 / root_signal, jnp.sqrt(signal_prev) - toward * root_signal / root_noise,
        toward / root_noise, spread, 1.0 / root_noise,
    )
    place = lax.broadcasted_iota(jnp.int32, (1, D), 1)
    row = jnp.zeros((1, D), f32)
    for i, value in enumerate(coefs):
        row = jnp.where(place == i, value, row)
    consts = jnp.concatenate([time_features(moment)[None], row], axis=0)
    vmem = pl.BlockSpec(memory_space=pltpu.VMEM)
    anywhere = pl.BlockSpec(memory_space=pl.ANY)
    V = pltpu.VMEM
    weights = lambda: [
        V((PIX, D), bf16), V((D, 3 * D), bf16), V((D, D), bf16), V((D, FF), bf16),
        V((FF, D), bf16), V((D, PIX), bf16),
    ]
    shape = jax.ShapeDtypeStruct((NZ, 32, 64), f32)
    base, scaled = pl.pallas_call(
        step_kernel,
        out_shape=(shape, shape),
        in_specs=[vmem] * 5 + [anywhere] * 16,
        out_specs=(anywhere, vmem),
        scratch_shapes=weights() + weights() + [
            V((1024, 2048), bf16), V((2, 256, 1024), f32), V((256, 512), bf16),
            V((512, 256), bf16), V((512, 512), bf16), V((256, 256), bf16),
            V((512, 512), bf16), V((256, 256), bf16), V((2, 256, 512), bf16),
            V((NZ, 32, 64), f32),
            V((4, 256, 128), f32), V((12, 32, 128), f32), V((512, 512), bf16),
            V((GY, 64, 256), bf16), V((GY, 64, 256), bf16), V((GY, 64, 256), bf16),
            V((GY, 64, 256), bf16), V((GY, 64, 256), bf16),
            V((GZ, 32, 256), f32), V((GZ, 32, 256), f32),
            V((HALF, PIX), bf16), V((HALF, D), f32), V((HALF, D), bf16),
            V((2 * HALF, 2 * D), bf16), V((PIX, HALF), f32), V((PARTS, PIX, CHUNK), bf16),
            V((PARTS, PIX, CHUNK), bf16),
            V((PIX, 2048), f32), V((512, 1024), bf16), V((512, 128), f32),
            V((GROUP, 2, 16, 128), bf16), V((GROUP, 2, 16, 128), bf16),
            V((12, 16, 128), f32), V((GROUP, 2, 16, 128), bf16), V((GROUP, 2, 16, 128), bf16),
            V((PIX, 2048), bf16), V((GROUP * 32, 128), f32), V((2, PIX, 256), bf16),
            V((2, PIX, 256), bf16), V((PIX, HALF), f32),
            V((GROUP, 16, 128), bf16), V((GROUP, 16, 128), bf16),
            V((2, GY, 2, 32, 128), f32), V((2, 512, 128), f32),
            pltpu.SemaphoreType.DMA((23,)), pltpu.SemaphoreType.DMA((8,)),
            pltpu.SemaphoreType.DMA((8,)), pltpu.SemaphoreType.DMA((PARTS + 2,)),
            pltpu.SemaphoreType.DMA((PARTS + 2,)), pltpu.SemaphoreType.REGULAR,
        ],
        compiler_params=pltpu.CompilerParams(
            collective_id=0, has_side_effects=True, vmem_limit_bytes=58 * MIB
        ),
    )(
        consts, norm_gain.transpose(1, 0, 2), noisy.reshape(256, LAT),
        measured.reshape(8, 32, 64), cap_index, noise.transpose(0, 2, 1),
        w_patch, w_qkv, w_out, w_up, w_down, w_unpatch, *(jnp.asarray(t) for t in tables()),
    )
    estimate = root_noise * scaled
    previous = base + (coefs[2] * root_noise) * scaled
    return (previous.transpose(0, 2, 1), estimate.transpose(0, 2, 1))


def solution(mesh):
    placed = (
        P("gz", "gy", None),
        P(None, "gy", "gz"),
        P(),
        P(None, None, "gz", "gy"),
        P(None, "gz", "gy"),
    ) + (P(),) * 7
    return jax.shard_map(
        local,
        mesh=mesh,
        in_specs=placed,
        out_specs=(P(None, "gy", "gz"), P(None, "gy", "gz")),
        check_vma=False,
    )
```

```python
import math

import jax
import jax.numpy as jnp
import numpy as np
from jax import lax
from jax.experimental import pallas as pl
from jax.experimental.pallas import tpu as pltpu
from jax.sharding import PartitionSpec as P

PATCH = 16
D = 384
HEADS = 6
FF = 1536
TRAIN_STEPS = 1000
STRIDE = 100
NZ = 64
LAT = 512
GZ = 16
GY = 8
NY = 4
GROUP = GZ * NY
SIDE = LAT // PATCH
HALF = SIDE * SIDE // 2
PIX = PATCH * PATCH
norm_eps = 1e-05
MIB = 1024 * 1024
f32 = jnp.float32
bf16 = jnp.bfloat16
MESH_ID = pl.DeviceIdType.MESH
NT = (((1,), (1,)), ((), ()))
TN = (((0,), (0,)), ((), ()))


def tables():
    parity, half_x, block_y = np.meshgrid(np.arange(2), np.arange(16), np.arange(32), indexing="ij")
    block_x = (2 * half_x + parity).reshape(-1)
    block_y = block_y.reshape(-1)
    by, bx = np.meshgrid(np.arange(32), np.arange(32), indexing="ij")
    by, bx = by.reshape(-1), bx.reshape(-1)
    turn = 2 * np.pi * ((block_y[:, None] * by[None] + block_x[:, None] * bx[None]) % 32) / 32
    coarse = np.concatenate([np.cos(turn), -np.sin(turn)], axis=1)
    xi, yi = np.meshgrid(np.arange(16), np.arange(16), indexing="ij")
    xi, yi = xi.reshape(-1), yi.reshape(-1)
    turn = 2 * np.pi * ((yi[:, None] * by[None] + xi[:, None] * bx[None]) % 512) / 512
    twist = np.stack([np.cos(turn), -np.sin(turn)]) / 32.0
    fine = np.zeros((2, 16, 4, 2, 2, 2, 256))
    for half in range(2):
        for quarter in range(4):
            for rest in range(2):
                ax = 8 * half + 2 * quarter + rest
                turn = 2 * np.pi * ((np.arange(16)[:, None] * yi[None] + ax * xi[None]) % 16) / 16
                fine[half, :, quarter, 0, rest, 0] = np.cos(turn)
                fine[half, :, quarter, 0, rest, 1] = np.sin(turn)
                fine[half, :, quarter, 1, rest, 0] = -np.sin(turn)
                fine[half, :, quarter, 1, rest, 1] = np.cos(turn)
    fine = fine.reshape(2, 256, 512) / 16.0
    to_bf = lambda a: a.astype(jnp.bfloat16)
    order = np.zeros((512, 512), np.float32)
    for gy in range(8):
        for hx in range(16):
            for yb in range(4):
                order[hx * 32 + gy * 4 + yb, gy * 64 + hx * 4 + yb] = 1.0
    swap = np.zeros((256, 256), np.float32)
    for y in range(16):
        for x in range(16):
            swap[x * 16 + y, y * 16 + x] = 1.0
    cast = np.zeros((512, 512), np.float32)
    for xb in range(32):
        for s in range(4):
            for yb in range(4):
                cast[(xb % 2) * 256 + s * 64 + (xb // 2) * 4 + yb, xb * 16 + s * 4 + yb] = 1.0
    deal = np.zeros((256, 256), np.float32)
    spill = np.zeros((2, 256, 512), np.float32)
    for x in range(4):
        for zb in range(4):
            for yb in range(32):
                row = (yb // 4) * 32 + (x % 2) * 16 + zb * 4 + yb % 4
                deal[row, (x % 2) * 128 + zb * 32 + yb] = 1.0
                spill[x // 2, row, zb * 128 + x * 32 + yb] = 1.0
    return (
        to_bf(coarse),
        twist.astype(np.float32),
        to_bf(fine),
        to_bf(np.ascontiguousarray(fine.transpose(0, 2, 1))),
        to_bf(order),
        to_bf(swap),
        to_bf(cast),
        to_bf(deal),
        to_bf(spill),
    )


def cumulative_alpha(moment):
    phase_angle = (moment / TRAIN_STEPS + 0.008) / 1.008 * (math.pi / 2.0)
    return jnp.cos(phase_angle) ** 2


def time_features(moment):
    half_width = D // 2
    frequency = jnp.exp(
        -math.log(10000.0) * jnp.arange(half_width).astype(jnp.float32) / half_width
    )
    angles = moment * frequency
    return jnp.concatenate([jnp.sin(angles), jnp.cos(angles)])


def dot(a, b, dims=None):
    if dims is None:
        return jnp.dot(a, b, preferred_element_type=f32)
    return lax.dot_general(a, b, dims, preferred_element_type=f32)


def norm(values, gain_row):
    average = jnp.mean(values, axis=-1, keepdims=True)
    centred = values - average
    variance = jnp.mean(centred * centred, axis=-1, keepdims=True)
    return (centred * lax.rsqrt(variance + norm_eps) * gain_row).astype(bf16)


def gelu(v):
    return 0.5 * v * (1.0 + jnp.tanh(math.sqrt(2.0 / math.pi) * (v + 0.044715 * (v * v * v))))


def exchange_blocks(arrays, width):
    arrays = list(arrays)
    lane = lax.broadcasted_iota(jnp.int32, arrays[0].shape, 1) // width
    step = 1
    while step < len(arrays):
        low = (lane // step) % 2 == 0
        for i in range(len(arrays)):
            if i & step == 0:
                a, b = arrays[i], arrays[i | step]
                arrays[i] = jnp.where(low, a, pltpu.roll(b, step * width, axis=1))
                arrays[i | step] = jnp.where(low, pltpu.roll(a, 128 - step * width, axis=1), b)
        step *= 2
    return arrays


def attention(queries, keys, values, left):
    outs = []
    for pair in range(HEADS // 2):
        lanes = slice(128 * pair, 128 * pair + 128)
        q, k, v = queries[:, lanes], keys[:, lanes], values[:, lanes]
        halves = []
        for which in range(2):
            q_one = jnp.where(left if which == 0 else ~left, q, jnp.zeros_like(q))
            scores = dot(q_one, k, NT)
            top = jnp.max(scores, axis=-1, keepdims=True)
            raised = jnp.exp(scores - top)
            total = jnp.sum(raised, axis=-1, keepdims=True)
            halves.append(dot(raised.astype(bf16), v) / total)
        outs.append(jnp.where(left, halves[0], halves[1]).astype(bf16))
    return jnp.concatenate(outs, axis=1)


def tail(hidden, attended, w_out, w_up, w_down, gain1, gain2):
    hidden = hidden + dot(attended, w_out[...])
    inner = gelu(dot(norm(hidden, gain1), w_up[...])).astype(bf16)
    hidden = hidden + dot(inner, w_down[...])
    return norm(hidden, gain2)


PARTS = 4
CHUNK = HALF // PARTS


def step_kernel(*refs):
    (
        consts, gains, noisy, measured, cap, h_noise,
        h_patch, h_qkv, h_out, h_up, h_down, h_unpatch,
        h_coarse, h_twist, h_fine, h_fine_t, h_order, h_swap, h_cast, h_deal, h_spill,
        base, scaled,
        patch0, qkv0, out0, up0, down0, unpatch0,
        patch1, qkv1, out1, up1, down1, unpatch1,
        coarse, twist, fine, fine_t, order, swap, cast, deal, spill,
        noise, strips, wide, cut, high_src, low_src, own_dst, oth_dst, low_dst, relay_src, relay_dst,
        tok, hidden, queries, pairs, guess, guess16, guess_dst,
        summed, turned, spread, line_src, line_dst,
        cells, fix_src, fix_dst, turned2, spread2, back_src, back_dst, blended,
        col_src, col_dst, final_src, final_dst,
        load_sem, send_sem, recv_sem, pair_send, pair_recv, ready,
    ) = refs
    gz, gy = lax.axis_index("gz"), lax.axis_index("gy")
    col, plane = gz // 2, lax.rem(gz, 2)
    mine = col * GY + gy
    me = gz * NY + lax.rem(gy, NY)
    keeps = plane == gy // NY
    partner = {"gz": 2 * col + 1 - plane}
    feat = consts[0:1, :]
    root_noise, inv_signal = consts[1:2, 0:1], consts[1:2, 1:2]

    plan = [
        (h_cast, cast), (h_swap, swap), (h_order, order), (h_patch.at[0], patch0),
        (h_qkv.at[0], qkv0), (h_out.at[0], out0), (h_up.at[0], up0), (h_down.at[0], down0),
        (h_unpatch.at[0], unpatch0), (h_coarse, coarse), (h_twist, twist),
        (h_fine.at[plane], fine), (h_fine_t.at[plane], fine_t),
        (h_patch.at[1], patch1), (h_qkv.at[1], qkv1), (h_out.at[1], out1), (h_up.at[1], up1),
        (h_down.at[1], down1), (h_unpatch.at[1], unpatch1), (h_deal, deal),
        (h_spill, spill), (h_noise, noise),
    ]
    loads = [
        pltpu.make_async_copy(src, dst, load_sem.at[i]) for i, (src, dst) in enumerate(plan)
    ]
    for load in loads:
        load.start()

    barrier = pltpu.get_barrier_semaphore()
    for core in range(2):
        for k in range(1 - core, GY):
            where = {"gz": 2 * col + lax.rem(plane + core, 2), "gy": lax.rem(gy + k, GY)}
            pl.semaphore_signal(barrier, inc=1, device_id=where, device_id_type=MESH_ID)
        for k in range(1, GZ // 2):
            where = {"gz": 2 * lax.rem(col + k, GZ // 2) + core}
            pl.semaphore_signal(barrier, inc=1, device_id=where, device_id_type=MESH_ID)

    def remote(src, dst, send, recv, where):
        return pltpu.make_async_remote_copy(
            src_ref=src, dst_ref=dst, send_sem=send, recv_sem=recv,
            device_id=where, device_id_type=MESH_ID,
        )

    def send(src, dst, which, to_gz, to_gy):
        here = jnp.logical_and(to_gz == gz, to_gy == gy)

        @pl.when(here)
        def _():
            pltpu.make_async_copy(src, dst, recv_sem.at[which]).start()

        @pl.when(jnp.logical_not(here))
        def _():
            where = {"gz": to_gz, "gy": to_gy}
            remote(src, dst, send_sem.at[which], recv_sem.at[which], where).start()

    for g in range(4):
        strips[g] = noisy[:, 128 * g : 128 * g + 128]
        for part in range(2):
            rows = [strips[g, pl.ds(8 * part + i, 16, stride=16), :] for i in range(8)]
            for i, block in enumerate(exchange_blocks(rows, 16)):
                high = block.astype(bf16)
                at = slice((8 * g + i) * 16, (8 * g + i) * 16 + 16)
                cut[at, 128 * part : 128 * part + 128] = high
                cut[at, 256 + 128 * part : 384 + 128 * part] = (
                    block - high.astype(f32)
                ).astype(bf16)
    loads[0].wait()
    sorted_rows = dot(cast[...], cut[...]).astype(bf16).reshape(GY, 64, 512)
    high_src[...] = sorted_rows[:, :, :256]
    low_src[...] = sorted_rows[:, :, 256:]

    pl.semaphore_wait(barrier, 2 * GY - 1 + GZ - 2)

    def send_patches(src, dst, which):
        for k in range(NY):
            slot = lax.rem(gy + k, NY)
            for half in range(2):
                send(
                    src.at[half * NY + slot], dst.at[gy], which, 2 * col + half,
                    plane * NY + slot,
                )

    send_patches(high_src, own_dst, 0)
    peers = []
    for k in range(1, GY):
        peer = lax.rem(gy + k, GY)
        where = {"gy": peer}
        peers.append((peer, where))
        pl.semaphore_signal(ready, inc=1, device_id=where, device_id_type=MESH_ID)

    for s in range(2):
        for g in range(4):
            part = noisy[128 * s : 128 * s + 128, 128 * g : 128 * g + 128].T
            relay_src[4 * g : 4 * g + 4, :, 128 * s : 128 * s + 128] = part.reshape(4, 32, 128)

    relay_dst[gz] = relay_src[gz]

    for a in range(12):
        wide[a, :, 0:64] = measured[a] if a < 8 else cap[a - 8].astype(f32)
        quarter = [wide[a, pl.ds(q, 8, stride=4), :] for q in range(4)]
        for r in range(2):
            cells[a, 8 * r : 8 * r + 8, :] = jnp.concatenate(
                [v[:, 32 * r : 32 * r + 32] for v in quarter], axis=1
            )

    for load in loads[1:9]:
        load.wait()
    unpatch0[...] = dot(unpatch0[...], swap[...]).astype(bf16)

    def gather(dst, src, s, r, count):
        part = pl.ds(0, count)
        del src
        pltpu.make_async_copy(dst.at[part], dst.at[part], recv_sem.at[r]).wait()

    gather(own_dst, None, 0, 0, GY)
    swap_own = remote(own_dst, oth_dst, send_sem.at[1], recv_sem.at[1], partner)
    swap_own.start()
    send_patches(low_src, low_dst, 6)

    @pl.loop(1, GZ)
    def _(k):
        peer = lax.rem(gz + k, GZ)
        remote(
            relay_src.at[peer], relay_dst.at[gz], send_sem.at[2], recv_sem.at[2], {"gz": peer}
        ).start()

    tok[...] = dot(order[...], own_dst[...].reshape(HALF, 256)).astype(bf16)

    def gain(m, r):
        return gains[r, m : m + 1, :]

    first = dot(tok[...], patch0[...]) + feat
    hidden[...] = first
    normed = norm(first, gain(0, 0))
    queries[...] = (dot(normed, qkv0[:, :D]).astype(bf16) * 0.125).astype(bf16)
    pairs[0:HALF, :] = dot(normed, qkv0[:, D:]).astype(bf16)
    swap_own.wait()
    normed = norm(dot(oth_dst[...].reshape(HALF, 256), patch0[...]) + feat, gain(0, 0))
    pairs[HALF:, :] = dot(normed, qkv0[:, D:]).astype(bf16)

    left = lax.broadcasted_iota(jnp.int32, (HALF, 128), 1) < 64
    attended = attention(queries[...], pairs[:, :D], pairs[:, D:], left)
    queries[...] = tail(hidden[...], attended, out0, up0, down0, gain(0, 1), gain(0, 2))
    summed[:, 0:HALF] = dot(swap[...], tok[...], NT)
    for i in range(PARTS):
        at = slice(i * CHUNK, i * CHUNK + CHUNK)
        net = dot(unpatch0[...], queries[at, :], (((0,), (1,)), ((), ())))
        first = (summed[:, at] - root_noise * net) * inv_signal
        guess[:, at] = first
        guess16[i] = first.astype(bf16)
        remote(
            guess16.at[i], guess_dst.at[i], pair_send.at[i], pair_recv.at[i], partner
        ).start()

    for load in loads[9:13]:
        load.wait()
    half_rows = pl.ds(pl.multiple_of(plane * HALF, HALF), HALF)
    side_rows = pl.ds(pl.multiple_of((1 - plane) * HALF, HALF), HALF)
    held = jnp.concatenate([guess16[i] for i in range(PARTS)], axis=1)
    for c in range(4):
        at = slice(512 * c, 512 * c + 512)
        summed[:, at] = dot(held, coarse[half_rows, at])
    for i in range(PARTS):
        remote(
            guess16.at[i], guess_dst.at[i], pair_send.at[i], pair_recv.at[i], partner
        ).wait()
    theirs = jnp.concatenate([guess_dst[i] for i in range(PARTS)], axis=1)
    for c in range(4):
        at = slice(256 * c, 256 * c + 256)
        im = slice(1024 + 256 * c, 1280 + 256 * c)
        real = summed[:, at] + dot(theirs, coarse[side_rows, at])
        imag = summed[:, im] + dot(theirs, coarse[side_rows, im])
        t_re, t_im = twist[0, :, at], twist[1, :, at]
        turned[0:256, at] = (real * t_re - imag * t_im).astype(bf16)
        turned[256:512, at] = (real * t_im + imag * t_re).astype(bf16)

    pl.semaphore_wait(ready, GY - 1)

    @pl.loop(0, 4)
    def _(i):
        block = lax.rem(i + gz // 4, 4)
        res = dot(fine[pl.ds(pl.multiple_of(block * 64, 64), 64), :], turned[...])
        for c in range(8):
            spread[pl.ds(c, 64, stride=8), :] = res[:, 128 * c : 128 * c + 128]
        line_src[pl.ds(block * 16, 16)] = spread[...].astype(bf16).reshape(16, 2, 16, 128)

        @pl.loop(0, 16)
        def _(j):
            peer = block * 16 + j

            send(
                line_src.at[peer], line_dst.at[mine], 3, peer // NY, plane * NY + lax.rem(peer, NY)
            )

    angle = cells[8:12] * (2.0 * math.pi / NZ)
    w_re, w_im = jnp.cos(angle), -jnp.sin(angle)
    turns = lax.rem(cells[8:12].astype(jnp.int32) * mine, NZ).astype(f32) * (2.0 * math.pi / NZ)
    first_re, first_im = jnp.cos(turns), jnp.sin(turns)
    gather(low_dst, None, 6, 6, GY)
    low = dot(order[...], low_dst[...].reshape(HALF, 256)).astype(bf16)
    guess[...] = guess[...] + dot(swap[...], low, NT) * inv_signal
    gather(line_dst, None, 3, 3, GROUP)

    def pick(i, state):
        p_re, p_im = state
        z = NZ - 1 - i
        x_re, x_im = line_dst[z, 0].astype(f32), line_dst[z, 1].astype(f32)
        return (
            p_re * w_re - p_im * w_im + x_re[None],
            p_re * w_im + p_im * w_re + x_im[None],
        )

    zero = jnp.zeros_like(w_re)
    p_re, p_im = lax.fori_loop(0, NZ, pick, (zero, zero), unroll=8)
    scale = 1.0 / math.sqrt(NZ)
    want = cells[0:8].reshape(4, 2, 16, 128)
    r_re = (want[:, 0] - p_re * scale) * scale
    r_im = (want[:, 1] - p_im * scale) * scale
    state = (r_re * first_re - r_im * first_im, r_re * first_im + r_im * first_re)

    def put(ref, z, state):
        t_re, t_im = state
        ref[z, 0] = (t_re[0] + t_re[1] + t_re[2] + t_re[3]).astype(bf16)
        ref[z, 1] = (t_im[0] + t_im[1] + t_im[2] + t_im[3]).astype(bf16)
        return (t_re * w_re + t_im * w_im, t_im * w_re - t_re * w_im)

    def expand(k, state):
        z = lax.rem(mine + k, NZ)
        state = put(fix_src, z, state)
        send(fix_src.at[z], fix_dst.at[me], 4, 2 * (z // GY) + gy // NY, lax.rem(z, GY))
        return state

    lax.fori_loop(0, GROUP, expand, state)

    gather(fix_dst, None, 4, 4, GROUP)
    spread2[...] = fix_dst[...].reshape(GROUP * 32, 128).astype(f32)
    for c in range(4):
        at = slice(c * 256, c * 256 + 256)
        block = jnp.concatenate(
            [spread2[pl.ds(2 * c + k, 256, stride=8), :].astype(bf16) for k in range(2)], axis=1
        )
        res = dot(fine_t[...], block)
        real, imag = res[:256], res[256:]
        t_re, t_im = twist[0, :, at], twist[1, :, at]
        turned2[:, at] = (real * t_re + imag * t_im).astype(bf16)
        turned2[:, 1024 + c * 256 : 1280 + c * 256] = (imag * t_re - real * t_im).astype(bf16)
    for c in range(2):
        rows = pl.ds(pl.multiple_of((1 - plane) * HALF + c * 256, 256), 256)
        back_src[c] = dot(turned2[...], coarse[rows, :], NT).astype(bf16)
        remote(
            back_src.at[c], back_dst.at[c], pair_send.at[PARTS + c], pair_recv.at[PARTS + c],
            partner,
        ).start()
    for c in range(2):
        rows = pl.ds(pl.multiple_of(plane * HALF + c * 256, 256), 256)
        at = slice(c * 256, c * 256 + 256)
        blended[:, at] = guess[:, at] + dot(turned2[...], coarse[rows, :], NT)
    for c in range(2):
        at = slice(c * 256, c * 256 + 256)
        remote(
            back_src.at[c], back_dst.at[c], pair_send.at[PARTS + c], pair_recv.at[PARTS + c],
            partner,
        ).wait()
        blended[:, at] = blended[:, at] + back_dst[c].astype(f32)

    for q in range(4):
        for g in range(4):
            rows = [
                blended[q * 64 + r * 16 : q * 64 + r * 16 + 16, 128 * g : 128 * g + 128]
                for r in range(4)
            ]
            for i, block in enumerate(exchange_blocks(rows, 32)):
                col_src[(4 * g + i) * 4 + q] = block.astype(bf16)

    @pl.loop(0, GROUP)
    def _(k):
        peer = lax.rem(me + k, GROUP)
        send(col_src.at[peer], col_dst.at[mine], 5, peer // NY, plane * NY + lax.rem(peer, NY))

    for load in loads[13:]:
        load.wait()
    gather(relay_dst, None, 2, 2, GZ - 1)
    c_old, c_new, inv_noise = consts[1:2, 3:4], consts[1:2, 4:5], consts[1:2, 5:6]

    @pl.loop(0, GZ)
    def _(i):
        for z in range(4):
            noise[4 * i + z] = (
                c_old * relay_dst[i, :, 64 * z : 64 * z + 64] + c_new * noise[4 * i + z]
            )

    store = pltpu.make_async_copy(noise, base, load_sem.at[len(plan)])
    store.start()

    patch1[...] = dot(swap[...], patch1[...]).astype(bf16)
    unpatch1[...] = dot(unpatch1[...], swap[...]).astype(bf16)
    gather(col_dst, None, 5, 5, GROUP)
    for zb in range(4):
        pix = col_dst[zb * 16 : zb * 16 + 16].reshape(256, 128)
        first = dot(pix, patch1[...], TN) + feat
        for x in range(4):
            hidden[x * 128 + zb * 32 : x * 128 + zb * 32 + 32, :] = first[32 * x : 32 * x + 32, :]
    normed = norm(hidden[...], gain(1, 0))
    queries[...] = (dot(normed, qkv1[:, :D]).astype(bf16) * 0.125).astype(bf16)
    pairs[0:HALF, :] = dot(normed, qkv1[:, D:]).astype(bf16)
    left1 = lax.broadcasted_iota(jnp.int32, (128, 128), 1) < 64
    for p in range(2):
        half = slice(256 * p, 256 * p + 256)
        attended = []
        for x in range(2):
            at = slice(256 * p + 128 * x, 256 * p + 128 * x + 128)
            attended.append(attention(queries[at, :], pairs[at, :D], pairs[at, D:], left1))
        attended = jnp.concatenate(attended, axis=0)
        normed = tail(hidden[half, :], attended, out1, up1, down1, gain(1, 1), gain(1, 2))
        moved = dot(deal[...], normed).astype(bf16)
        value = jnp.zeros((256, 256), f32)
        for zb in range(4):
            pix = col_dst[zb * 16 : zb * 16 + 16].reshape(256, 128)
            value = value + dot(spill[p, :, 128 * zb : 128 * zb + 128], pix, NT)
        value = value * inv_noise + dot(moved, unpatch1[...])
        for h in range(2):
            final_src[p, :, h] = value[:, 128 * h : 128 * h + 128].reshape(GY, 32, 128)
        here = pl.ds(pl.multiple_of(gy * 64 + p * 32, 32), 32)
        for peer, where in peers:
            remote(
                final_src.at[p, peer], final_dst.at[:, here, :], send_sem.at[7], recv_sem.at[7],
                where,
            ).start()
        final_dst[:, here, :] = final_src[p, gy]

    def drain(src, which, count):
        part = pl.ds(0, count)
        pltpu.make_async_copy(src.at[part], src.at[part], send_sem.at[which]).wait()

    def drain_kept(kept):
        drain(high_src, 0, GY - kept)
        drain(low_src, 6, GY - kept)
        drain(line_src, 3, GROUP - kept)
        drain(fix_src, 4, GROUP - kept)
        drain(col_src, 5, GROUP - kept)

    @pl.when(keeps)
    def _():
        drain_kept(1)

    @pl.when(jnp.logical_not(keeps))
    def _():
        drain_kept(0)

    drain(relay_src, 2, GZ - 1)
    done = final_dst.at[:, pl.ds(0, (GY - 1) * 64), :]
    pltpu.make_async_copy(done, done, send_sem.at[7]).wait()
    pltpu.make_async_copy(done, done, recv_sem.at[7]).wait()

    for g in range(4):
        at = slice(8 * g, 8 * g + 8)
        for zb in range(4):
            for h in range(2):
                blocks = [
                    final_dst[h, pl.ds(128 * g + zb * 4 + yb, 8, stride=16), :] for yb in range(4)
                ]
                for i, block in enumerate(exchange_blocks(blocks, 16)):
                    for part in range(2):
                        z = zb * 16 + h * 8 + part * 4 + i
                        value = block[:, 64 * part : 64 * part + 64]
                        scaled[z, at, :] = value
    store.wait()


def local(
    noisy, noise, timestep, measured, cap_index, w_patch, w_qkv, w_out, w_up, w_down, w_unpatch,
    norm_gain,
):
    moment = timestep[0].astype(f32)
    signal_now = cumulative_alpha(moment)
    signal_prev = cumulative_alpha(moment - STRIDE)
    root_signal = jnp.sqrt(signal_now)
    root_noise = jnp.sqrt(1.0 - signal_now)
    toward = jnp.sqrt(
        (1.0 - signal_prev) * signal_now * (1.0 / signal_prev - 1.0) / (1.0 - signal_now)
    )
    spread = jnp.sqrt((1.0 - signal_prev) / (1.0 - signal_now) * (1.0 - signal_now / signal_prev))
    coefs = (
        root_noise, 1.0 / root_signal, jnp.sqrt(signal_prev) - toward * root_signal / root_noise,
        toward / root_noise, spread, 1.0 / root_noise,
    )
    place = lax.broadcasted_iota(jnp.int32, (1, D), 1)
    row = jnp.zeros((1, D), f32)
    for i, value in enumerate(coefs):
        row = jnp.where(place == i, value, row)
    consts = jnp.concatenate([time_features(moment)[None], row], axis=0)
    vmem = pl.BlockSpec(memory_space=pltpu.VMEM)
    anywhere = pl.BlockSpec(memory_space=pl.ANY)
    V = pltpu.VMEM
    weights = lambda: [
        V((PIX, D), bf16), V((D, 3 * D), bf16), V((D, D), bf16), V((D, FF), bf16),
        V((FF, D), bf16), V((D, PIX), bf16),
    ]
    shape = jax.ShapeDtypeStruct((NZ, 32, 64), f32)
    base, scaled = pl.pallas_call(
        step_kernel,
        out_shape=(shape, shape),
        in_specs=[vmem] * 5 + [anywhere] * 16,
        out_specs=(anywhere, vmem),
        scratch_shapes=weights() + weights() + [
            V((1024, 2048), bf16), V((2, 256, 1024), f32), V((256, 512), bf16),
            V((512, 256), bf16), V((512, 512), bf16), V((256, 256), bf16),
            V((512, 512), bf16), V((256, 256), bf16), V((2, 256, 512), bf16),
            V((NZ, 32, 64), f32),
            V((4, 256, 128), f32), V((12, 32, 128), f32), V((512, 512), bf16),
            V((GY, 64, 256), bf16), V((GY, 64, 256), bf16), V((GY, 64, 256), bf16),
            V((GY, 64, 256), bf16), V((GY, 64, 256), bf16),
            V((GZ, 32, 256), f32), V((GZ, 32, 256), f32),
            V((HALF, PIX), bf16), V((HALF, D), f32), V((HALF, D), bf16),
            V((2 * HALF, 2 * D), bf16), V((PIX, HALF), f32), V((PARTS, PIX, CHUNK), bf16),
            V((PARTS, PIX, CHUNK), bf16),
            V((PIX, 2048), f32), V((512, 1024), bf16), V((512, 128), f32),
            V((GROUP, 2, 16, 128), bf16), V((GROUP, 2, 16, 128), bf16),
            V((12, 16, 128), f32), V((GROUP, 2, 16, 128), bf16), V((GROUP, 2, 16, 128), bf16),
            V((PIX, 2048), bf16), V((GROUP * 32, 128), f32), V((2, PIX, 256), bf16),
            V((2, PIX, 256), bf16), V((PIX, HALF), f32),
            V((GROUP, 16, 128), bf16), V((GROUP, 16, 128), bf16),
            V((2, GY, 2, 32, 128), f32), V((2, 512, 128), f32),
            pltpu.SemaphoreType.DMA((23,)), pltpu.SemaphoreType.DMA((8,)),
            pltpu.SemaphoreType.DMA((8,)), pltpu.SemaphoreType.DMA((PARTS + 2,)),
            pltpu.SemaphoreType.DMA((PARTS + 2,)), pltpu.SemaphoreType.REGULAR,
        ],
        compiler_params=pltpu.CompilerParams(
            collective_id=0, has_side_effects=True, vmem_limit_bytes=58 * MIB
        ),
    )(
        consts, norm_gain.transpose(1, 0, 2), noisy.reshape(256, LAT),
        measured.reshape(8, 32, 64), cap_index, noise.transpose(0, 2, 1),
        w_patch, w_qkv, w_out, w_up, w_down, w_unpatch, *(jnp.asarray(t) for t in tables()),
    )
    estimate = root_noise * scaled
    previous = base + (coefs[2] * root_noise) * scaled
    return (previous.transpose(0, 2, 1), estimate.transpose(0, 2, 1))


def solution(mesh):
    placed = (
        P("gz", "gy", None),
        P(None, "gy", "gz"),
        P(),
        P(None, None, "gz", "gy"),
        P(None, "gz", "gy"),
    ) + (P(),) * 7
    return jax.shard_map(
        local,
        mesh=mesh,
        in_specs=placed,
        out_specs=(P(None, "gy", "gz"), P(None, "gy", "gz")),
        check_vma=False,
    )
```
